32 devices in a mesh: dp: 8 (over y, x, core), tensor: 4 (over z).
Axes of the slice: x: 2, y: 2, z: 4, core: 2. Of those that a mesh axis runs over, the one named last changes fastest.
Arguments:
- tokens: bfloat16 [8192, 1024], P(('dp', 'tensor')), may hold values from -6 to 6
- cotangent: bfloat16 [8192, 1024], P(('dp', 'tensor')), may hold values from -6 to 6
- doc_lengths: int32 [8, 8], P('dp'), may hold values from 1 to 832, 1024 in all within a row
- query_weight: bfloat16 [1024, 1024], P('dp', 'tensor'), may hold values from -0.1875 to 0.1875
- key_weight: bfloat16 [1024, 1024], P('dp', 'tensor'), may hold values from -0.1875 to 0.1875
- value_weight: bfloat16 [1024, 1024], P('dp', 'tensor'), may hold values from -0.1875 to 0.1875
- output_weight: bfloat16 [1024, 1024], P('tensor', 'dp'), may hold values from -3 to 3
- inner_weight: bfloat16 [1024, 4096], P('dp', 'tensor'), may hold values from -0.1875 to 0.1875
- outer_weight: bfloat16 [4096, 1024], P('tensor', 'dp'), may hold values from -0.09375 to 0.09375
- query_offset: bfloat16 [1024], P(('tensor', 'dp')), may hold values from -3 to 3
- value_offset: bfloat16 [1024], P(('tensor', 'dp')), may hold values from -3 to 3
- inner_offset: bfloat16 [4096], P(('tensor', 'dp')), may hold values from -3 to 3
- output_offset: bfloat16 [1024], P(('dp', 'tensor')), may hold values from -3 to 3
- outer_offset: bfloat16 [1024], P(('dp', 'tensor')), may hold values from -3 to 3
- first_gain: bfloat16 [1024], P(('dp', 'tensor')), may hold values from 0.25 to 1.75
- first_shift: bfloat16 [1024], P(('dp', 'tensor')), may hold values from -3 to 3
- second_gain: bfloat16 [1024], P(('dp', 'tensor')), may hold values from 0.25 to 1.75
- second_shift: bfloat16 [1024], P(('dp', 'tensor')), may hold values from -3 to 3
Outputs:
- layer_out: bfloat16 [8192, 1024], P(('dp', 'tensor'))
- tokens_grad: float32 [8192, 1024], P(('dp', 'tensor'))
- query_grad: float32 [1024, 1024], P('dp', 'tensor')
- key_grad: float32 [1024, 1024], P('dp', 'tensor')
- value_grad: float32 [1024, 1024], P('dp', 'tensor')
- output_grad: float32 [1024, 1024], P('tensor', 'dp')
- inner_grad: float32 [1024, 4096], P('dp', 'tensor')
- outer_grad: float32 [4096, 1024], P('tensor', 'dp')
- offset_query: float32 [1024], P(('tensor', 'dp'))
- offset_value: float32 [1024], P(('tensor', 'dp'))
- offset_inner: float32 [4096], P(('tensor', 'dp'))
- offset_output: float32 [1024], P(('dp', 'tensor'))
- offset_outer: float32 [1024], P(('dp', 'tensor'))
- gain_first: float32 [1024], P(('dp', 'tensor'))
- shift_first: float32 [1024], P(('dp', 'tensor'))
- gain_second: float32 [1024], P(('dp', 'tensor'))
- shift_second: float32 [1024], P(('dp', 'tensor'))
The draws below stay inside these ranges and needn't reach their ends.
Inputs may be any that keep to these rules, and one draw needn't show every extreme that they name: `doc_lengths`: row s lists, in order, the lengths of the 8 documents packed into sequence s; they sum to 1024, and the longest has exactly 832 tokens.
All inputs are finite; a program needn't handle non-finite values.
Results may differ from the reference program's by a relative error of at most 0.018.
Values may be sent and summed in bfloat16 or wider, within the bound.
No kernel may reach another device: no remote copies, remote signals or barrier semaphores. Data moves between devices by JAX's collectives and lax.ppermute only.
A program may use at most 128 MiB of HBM per device.

```python
import math
import jax
import jax.numpy as jnp
import numpy as np
from jax import lax

D = 1024
HEADS = 16
HEAD_DIM = 64
FF = 4096
LENGTH = 1024
DOCS = 8
NSEQ = 8
TOKENS = 8192


def shard_levels(key, dims, pieces, low, high):
    level = 1.0
    for position, parts in pieces:
        draws = jax.random.uniform(jax.random.fold_in(jax.random.fold_in(key, 6), position), (parts,), jnp.float32, low / len(pieces), high / len(pieces))
        level = level * jnp.repeat(jnp.exp(draws), dims[position] // parts).reshape((-1,) + (1,) * (len(dims) - 1 - position))
    return level


def length_profile(count, total, limit, slope):
    portions = [(1 << 20) // math.isqrt(grade ** slope) + 1 for grade in range(2, count + 1)]
    surplus, counts = total - limit - (count - 1), [1] * (count - 1)
    while surplus > 0:
        candidates = [i for i in range(count - 1) if counts[i] < limit]
        pool, remaining = sum([portions[i] for i in candidates]), surplus
        for i in candidates:
            extra = min(limit - counts[i], max(1, remaining * portions[i] // pool), surplus)
            counts[i] = counts[i] + extra
            surplus = surplus - extra
    return np.array([limit] + counts)


def uneven(own_key, number_of, total, limit, lean):
    if number_of == 2:
        one = jax.random.randint(own_key, (), max(1, total - limit), min(limit, total - 1) + 1)
        return jnp.stack([one, total - one])
    tallies = jnp.asarray(length_profile(number_of, total, limit, lean), jnp.int32)
    twos = (number_of - 1) // 2
    donor, receiver = tallies[1:1 + 2 * twos:2], tallies[2:2 + 2 * twos:2]
    room = jnp.minimum(donor - 1, limit - receiver)
    moved = jax.random.randint(jax.random.fold_in(own_key, 1), (twos,), 0, 1 << 20) % (room + 1)
    tallies = tallies.at[1:1 + 2 * twos:2].set(donor - moved).at[2:2 + 2 * twos:2].set(receiver + moved)
    return tallies[jax.random.permutation(jax.random.fold_in(own_key, 2), number_of)]


def normal_values(rng, shape, spread, bound, split=(), held_as=jnp.bfloat16):
    drawn = jax.random.normal(rng, shape, jnp.float32) * spread
    if len(split) > 0:
        drawn = shard_levels(rng, shape, split, -0.22, 0.18) * drawn
    return jnp.clip(drawn, min=-bound, max=bound).astype(held_as)


def setup_inputs(seed: int = 0) -> dict:
    key_list = jax.random.split(jax.random.key(seed), 19)
    return {
        "tokens": normal_values(key_list[0], (TOKENS, D), 1.0, 6.0, ((0, 32),)),
        "cotangent": normal_values(key_list[1], (TOKENS, D), 1.0, 6.0, ((0, 32),)),
        "doc_lengths": jax.vmap(lambda own: uneven(own, DOCS, LENGTH, LENGTH * 13 // 16, 0))(jax.random.split(key_list[2], NSEQ)).reshape((NSEQ, DOCS)).astype(jnp.int32),
        "query_weight": normal_values(key_list[3], (D, D), D ** -0.5, 0.1875, ((0, 8), (1, 4))),
        "key_weight": normal_values(key_list[4], (D, D), D ** -0.5, 0.1875, ((0, 8), (1, 4))),
        "value_weight": normal_values(key_list[5], (D, D), D ** -0.5, 0.1875, ((0, 8), (1, 4))),
        "output_weight": normal_values(key_list[6], (D, D), (D * 4 // LENGTH) ** -0.5, 3.0, ((0, 4), (1, 8))),
        "inner_weight": normal_values(key_list[7], (D, FF), D ** -0.5, 0.1875, ((0, 8), (1, 4))),
        "outer_weight": normal_values(key_list[8], (FF, D), FF ** -0.5, 0.09375, ((0, 4), (1, 8))),
        "query_offset": normal_values(key_list[9], (D,), 0.5, 3.0, ((0, 32),)),
        "value_offset": normal_values(key_list[10], (D,), 0.5, 3.0, ((0, 32),)),
        "inner_offset": normal_values(key_list[11], (FF,), 0.5, 3.0, ((0, 32),)),
        "output_offset": normal_values(key_list[12], (D,), 0.5, 3.0, ((0, 32),)),
        "outer_offset": normal_values(key_list[13], (D,), 0.5, 3.0, ((0, 32),)),
        "first_gain": jnp.clip(1.0 + 0.15 * jax.random.normal(key_list[14], (D,), jnp.float32), 0.25, 1.75).astype(jnp.bfloat16),
        "first_shift": normal_values(key_list[15], (D,), 0.5, 3.0, ((0, 32),)),
        "second_gain": jnp.clip(1.0 + 0.15 * jax.random.normal(key_list[16], (D,), jnp.float32), 0.25, 1.75).astype(jnp.bfloat16),
        "second_shift": normal_values(key_list[17], (D,), 0.5, 3.0, ((0, 32),)),
    }


@jax.custom_vjp
def low(v):
    return lax.optimization_barrier(v.astype(jnp.bfloat16)).astype(jnp.float32)

@jax.custom_vjp
def low_back(v):
    return v

def low_keep(v):
    return (low(v), None)

def low_pass(kept, grad):
    return (grad,)

def back_keep(v):
    return (v, None)

def back_low(kept, grad):
    return (low(grad),)
low.defvjp(low_keep, low_pass)
low_back.defvjp(back_keep, back_low)

def matmul(left, right):
    return jnp.dot(left, right, precision=lax.Precision.HIGHEST)

def norm_rows(value, gain, shift):
    centered = value - lax.optimization_barrier(jnp.mean(value, -1, keepdims=True))
    scale = lax.rsqrt(lax.optimization_barrier(jnp.mean(centered * centered, -1, keepdims=True)) + 1e-05)
    return centered * scale * gain + shift

def block_attend(queries, keys, values, own, segment):
    scores = low_back(jnp.einsum('qhd,khd->hqk', queries, keys, precision=lax.Precision.HIGHEST) * 0.125)
    same = (own[:, None] == segment[None, :])[None]
    scores = jnp.where(same, scores, -1e+30)
    top = lax.optimization_barrier(jnp.max(scores, -1, keepdims=True))
    expo = jnp.exp(scores - top)
    shares = low(expo / lax.optimization_barrier(jnp.sum(expo, -1, keepdims=True)))
    return jnp.einsum('hqk,khd->qhd', shares, values, precision=lax.Precision.HIGHEST)

def sequence_attend(item):
    queries, keys, values, segment = item
    block = min(512, LENGTH)
    count = LENGTH // block
    query_blocks = queries.reshape(count, block, HEADS, HEAD_DIM)
    owners = segment.reshape(count, block)
    runner = jax.checkpoint(lambda pair: block_attend(pair[0], keys, values, pair[1], segment))
    return lax.map(runner, (query_blocks, owners)).reshape(LENGTH, HEADS, HEAD_DIM)

def layer(tokens, query_weight, key_weight, value_weight, output_weight, inner_weight, outer_weight, query_offset, value_offset, inner_offset, output_offset, outer_offset, first_gain, first_shift, second_gain, second_shift, segment):
    number = segment.shape[0]
    shape = (number, LENGTH, HEADS, HEAD_DIM)
    queries = low(low_back(matmul(tokens, query_weight) + query_offset)).reshape(shape)
    keys = low(low_back(matmul(tokens, key_weight))).reshape(shape)
    values = low(low_back(matmul(tokens, value_weight) + value_offset)).reshape(shape)
    mixed = lax.map(jax.checkpoint(sequence_attend), (queries, keys, values, segment))
    mixed = low(low_back(mixed.reshape(-1, D)))
    hidden = norm_rows(tokens + low_back(matmul(mixed, output_weight)) + output_offset, first_gain, first_shift)
    inner = low_back(matmul(low(hidden), inner_weight) + inner_offset)
    active = low(jax.nn.gelu(inner, approximate=False))
    return norm_rows(hidden + low_back(matmul(active, outer_weight)) + outer_offset, second_gain, second_shift)

def reference(tokens, cotangent, doc_lengths, query_weight, key_weight, value_weight, output_weight, inner_weight, outer_weight, query_offset, value_offset, inner_offset, output_offset, outer_offset, first_gain, first_shift, second_gain, second_shift):
    params = tuple((weight.astype(jnp.float32) for weight in (query_weight, key_weight, value_weight, output_weight, inner_weight, outer_weight, query_offset, value_offset, inner_offset, output_offset, outer_offset, first_gain, first_shift, second_gain, second_shift)))
    bounds = jnp.cumsum(doc_lengths, axis=1).astype(jnp.int32)
    places = jnp.arange(LENGTH, dtype=jnp.int32)
    segment = lax.optimization_barrier(jnp.sum((places[None, :, None] >= bounds[:, None, :]).astype(jnp.int32), -1)).astype(jnp.int32)
    total = doc_lengths.shape[0]
    group = math.gcd(total, max(1, 4096 // LENGTH))
    turns = total // group
    inputs = tokens.astype(jnp.float32).reshape(turns, group * LENGTH, D)
    upstreams = cotangent.astype(jnp.float32).reshape(turns, group * LENGTH, D)
    segments = segment.reshape(turns, group, LENGTH)

    def advance(carry, item):
        piece, upstream, segment_rows = item
        result, pull = jax.vjp(lambda given, *weights: layer(given, *weights, segment_rows), piece, *params)
        grads = pull(upstream)
        return (tuple((acc + grad for acc, grad in zip(carry, grads[1:]))), (result.astype(jnp.bfloat16), grads[0]))
    start = tuple((jnp.zeros(weight.shape, jnp.float32) for weight in params))
    sums, (outputs, token_grads) = lax.scan(advance, start, (inputs, upstreams, segments))
    return (outputs.reshape(-1, D), token_grads.reshape(-1, D), sums[0], sums[1], sums[2], sums[3], sums[4], sums[5], sums[6], sums[7], sums[8], sums[9], sums[10], sums[11], sums[12], sums[13], sums[14])
```

```python
import jax
import jax.numpy as jnp
from jax import lax
from jax.experimental import pallas as pl
from jax.experimental.pallas import tpu as pltpu
from jax.sharding import PartitionSpec as P

HEAD_DIM = 64
LENGTH = 1024
QUARTERS = 4
BLOCK = 256
HALF = 128
bf16 = jnp.bfloat16
f32 = jnp.float32
VMEM = pl.BlockSpec(memory_space=pltpu.VMEM)
SMEM = pl.BlockSpec(memory_space=pltpu.SMEM)
HBM = pl.BlockSpec(memory_space=pl.ANY)


def shape(dims, dtype):
    return jax.ShapeDtypeStruct(dims, dtype)


def call(kernel, name, operands, specs, outs, flops, scratch=(), moved=4 << 20, grid=()):
    return pl.pallas_call(
        kernel,
        grid=grid,
        name=name,
        out_shape=outs,
        in_specs=specs,
        out_specs=[VMEM] * len(outs),
        scratch_shapes=list(scratch),
        compiler_params=pltpu.CompilerParams(vmem_limit_bytes=52 << 20),
        cost_estimate=pl.CostEstimate(flops=flops, bytes_accessed=moved, transcendentals=0),
    )(*operands)


def dot(left, right, dims=((1,), (0,))):
    return lax.dot_general(left, right, (dims, ((), ())), preferred_element_type=f32)


NT = ((1,), (1,))
TN = ((0,), (0,))


def norm_back(grad, normed, scale, gain):
    scaled = grad * gain
    return scale * (
        scaled
        - jnp.mean(scaled, -1, keepdims=True)
        - normed * jnp.mean(scaled * normed, -1, keepdims=True)
    )


def lanes(ids, j):
    return pl.ds(pl.multiple_of((ids[0] ^ j) * BLOCK, BLOCK), BLOCK)


def segments(ids, docs, dims, axis):
    place = lax.broadcasted_iota(jnp.int32, dims, axis)
    place = ((ids[2] - (place >> 8) + QUARTERS) & (QUARTERS - 1)) * BLOCK + (place & (BLOCK - 1))
    bound = docs[0, 0]
    total = (place >= bound).astype(jnp.int32)
    for j in range(1, 8):
        bound = bound + docs[0, j]
        total = total + (place >= bound).astype(jnp.int32)
    return total


def attend_kernel(ids, docs, t0, t1, t2, t3, own, other, qb, vb, q, k, v, w, m0, m1, m2, m3, lse):
    core = ids[1]
    for j in range(4):
        base = (ids[0] ^ j) * BLOCK
        for source, side in ((own, core), (other, 1 - core)):
            rows = pl.ds(pl.multiple_of(base + side * HALF, HALF), HALF)
            for i in range(3):
                at = (j * 3 + i) * HALF
                w[rows, i * BLOCK : (i + 1) * BLOCK] = source[at : at + HALF, :]
    for b, t in enumerate((t0, t1, t2, t3)):
        rows = slice(b * BLOCK, (b + 1) * BLOCK)
        made = dot(t[...], w[...])
        q[rows, :] = (made[:, :BLOCK] + qb[...]).astype(bf16)
        k[rows, :] = made[:, BLOCK : 2 * BLOCK].astype(bf16)
        v[rows, :] = (made[:, 2 * BLOCK :] + vb[...]).astype(bf16)
    along = segments(ids, docs, (1, LENGTH), 1)
    down = segments(ids, docs, (LENGTH, 1), 0)
    for b, mixed in enumerate((m0, m1, m2, m3)):
        rows = slice(b * BLOCK, (b + 1) * BLOCK)
        same = down[rows] == along
        for h in range(4):
            cols = slice(h * HEAD_DIM, (h + 1) * HEAD_DIM)
            scores = dot(q[rows, cols] * bf16(0.125), k[:, cols], NT)
            scores = jnp.where(same, scores, -1e30)
            top = jnp.max(scores, -1, keepdims=True)
            expo = jnp.exp(scores - top)
            total = jnp.sum(expo, -1, keepdims=True)
            shares = (expo * (1.0 / total)).astype(bf16)
            mixed[:, cols] = dot(shares, v[:, cols]).astype(bf16)
            lse[rows, h : h + 1] = top + jnp.log(total)


def project_kernel(ids, tokens, x0, x1, x2, x3, *refs):
    own = refs[:16]
    other, bias, gain, shift, wo, normed, scale, low = refs[16:]
    core = ids[1]
    for k in range(4):
        for j in range(4):
            i = k * 4 + j
            mine = pl.ds(pl.multiple_of(k * BLOCK + core * HALF, HALF), HALF)
            theirs = pl.ds(pl.multiple_of(k * BLOCK + (1 - core) * HALF, HALF), HALF)
            wo[mine, lanes(ids, j)] = own[i][...]
            wo[theirs, lanes(ids, j)] = other[i * HALF : (i + 1) * HALF, :]
    total = tokens[...].astype(f32) + bias[...]
    for k, x in enumerate((x0, x1, x2, x3)):
        total = total + dot(x[...], wo[k * BLOCK : (k + 1) * BLOCK, :])
    centered = total - jnp.mean(total, -1, keepdims=True)
    r = lax.rsqrt(jnp.mean(centered * centered, -1, keepdims=True) + 1e-05)
    n = centered * r
    normed[...] = n
    scale[...] = jnp.broadcast_to(r, scale.shape)
    low[...] = (n * gain[...] + shift[...]).astype(bf16)


def fetch(blocks, held, sems):
    copies = [
        pltpu.make_async_copy(b.at[pl.ds(0, 1024)], held.at[i], sems.at[i])
        for i, b in enumerate(blocks)
    ]
    for copy in copies:
        copy.start()
    return copies


def forward_kernel(ids, mine, theirs, bias, *refs):
    blocks = refs[:16]
    active, slope, out_mine, out_theirs, held, rows, sems = refs[16:]
    copies = fetch(blocks, held, sems)
    rows[:BLOCK, :] = mine[...]
    rows[BLOCK:, :] = theirs[...]
    for k in range(4):
        for j in range(4):
            copies[k * 4 + j].wait()
        at = ((ids[2] - k + QUARTERS) & (QUARTERS - 1)) * 2 + ids[1]
        offset = bias[pl.ds(at, 1), :]
        for half in range(2):
            span = slice(half * BLOCK, (half + 1) * BLOCK)
            inner = jnp.broadcast_to(offset[:, span], (512, BLOCK))
            for j in range(4):
                inner = inner + dot(rows[:, lanes(ids, j)], held[k * 4 + j, span, :])
            phi = 0.5 * (1.0 + lax.erf(inner * 0.7071067811865476))
            active[k * 512 : (k + 1) * 512, span] = (inner * phi).astype(bf16)
            slope[k * 512 : (k + 1) * 512, span] = (
                phi + inner * jnp.exp(-0.5 * inner * inner) * 0.3989422804014327
            ).astype(bf16)
        for j in range(4):
            made = dot(active[k * 512 : (k + 1) * 512, :], held[k * 4 + j, 512:1024, :])
            at = lanes(ids, j)
            if k == 0:
                out_mine[:, at] = made[:BLOCK]
                out_theirs[:, at] = made[BLOCK:]
            else:
                out_mine[:, at] += made[:BLOCK]
                out_theirs[:, at] += made[BLOCK:]


def second_kernel(normed, gain1, shift1, mine, got, bias, gain, shift, cot, out, grad, low, sums):
    total = normed[...] * gain1[...] + shift1[...] + (mine[...] + got[...]) + bias[...]
    centered = total - jnp.mean(total, -1, keepdims=True)
    r = lax.rsqrt(jnp.mean(centered * centered, -1, keepdims=True) + 1e-05)
    n = centered * r
    out[...] = (n * gain[...] + shift[...]).astype(bf16)
    up = cot[...].astype(f32)
    back = norm_back(up, n, r, gain[...])
    grad[...] = back
    low[...] = back.astype(bf16)
    sums[0:1, :] = jnp.sum(back, 0, keepdims=True)
    sums[1:2, :] = jnp.sum(up * n, 0, keepdims=True)
    sums[2:3, :] = jnp.sum(up, 0, keepdims=True)


def backward_kernel(ids, mine, theirs, slope, *refs):
    blocks = refs[:16]
    back, out_mine, out_theirs, sums, held, rows, total, sems = refs[16:]
    copies = fetch(blocks, held, sems)
    rows[:BLOCK, :] = mine[...]
    rows[BLOCK:, :] = theirs[...]
    sums[...] = jnp.zeros(sums.shape, f32)
    for k in range(4):
        for j in range(4):
            copies[k * 4 + j].wait()
        span = slice(k * 512, (k + 1) * 512)
        made = dot(rows[:, lanes(ids, 0)], held[k * 4, 512:1024, :], NT)
        for j in range(1, 4):
            made = made + dot(rows[:, lanes(ids, j)], held[k * 4 + j, 512:1024, :], NT)
        made = (made * slope[span, :].astype(f32)).astype(bf16)
        back[span, :] = made
        at = ((ids[2] - k + QUARTERS) & (QUARTERS - 1)) * 2 + ids[1]
        sums[pl.ds(at, 1), :] = jnp.sum(made.astype(f32), 0, keepdims=True)
        for j in range(4):
            part = dot(made[:, :BLOCK], held[k * 4 + j, :BLOCK, :], NT) + dot(
                made[:, BLOCK:], held[k * 4 + j, BLOCK:512, :], NT
            )
            at = lanes(ids, j)
            if k == 0:
                total[:, at] = part
            else:
                total[:, at] += part
    out_mine[...] = total[:BLOCK, :]
    out_theirs[...] = total[BLOCK:, :].astype(bf16)


def weights_kernel(ids, active, back, mine, theirs, gmine, gtheirs, o0, o1, o2, o3):
    for j, out in enumerate((o0, o1, o2, o3)):
        at = lanes(ids, j)
        left = dot(mine[:, at], back[:BLOCK, :], TN) + dot(theirs[:, at], back[BLOCK:, :], TN)
        out[:BLOCK, :] = left[:, :BLOCK].astype(bf16)
        out[BLOCK:512, :] = left[:, BLOCK:].astype(bf16)
        out[512:1024, :] = (
            dot(active[:BLOCK, :], gmine[:, at], TN) + dot(active[BLOCK:, :], gtheirs[:, at], TN)
        ).astype(bf16)


def first_kernel(second, mine, got, normed, scale, gain, wo, grad, low, g0, g1, g2, g3, sums):
    hidden = second[...] + mine[...] + got[...].astype(f32)
    n = normed[...]
    back = norm_back(hidden, n, scale[:, :1], gain[...])
    grad[...] = back
    rounded = back.astype(bf16)
    low[...] = rounded
    for k, g in enumerate((g0, g1, g2, g3)):
        g[...] = dot(rounded, wo[k * BLOCK : (k + 1) * BLOCK, :], NT).astype(bf16)
    sums[0:1, :] = jnp.sum(back, 0, keepdims=True)
    sums[1:2, :] = jnp.sum(hidden * n, 0, keepdims=True)
    sums[2:3, :] = jnp.sum(hidden, 0, keepdims=True)


def output_grad_kernel(ids, x0, x1, x2, x3, low, own, send, made):
    core = ids[1]
    for k, x in enumerate((x0, x1, x2, x3)):
        made[...] = dot(x[...], low[...], TN)
        for out, side in ((own, core), (send, 1 - core)):
            rows = pl.ds(pl.multiple_of(side * HALF, HALF), HALF)
            for j in range(4):
                at = j * 512 + k * HALF
                out[at : at + HALF, :] = made[rows, lanes(ids, j)].astype(bf16)


def attend_back_kernel(
    ids, docs, q, k, v, lse, g0, g1, g2, g3, w, d0, d1, d2, d3, dqkv, sums, g, ktot, vtot
):
    for b, part in enumerate((g0, g1, g2, g3)):
        g[b * BLOCK : (b + 1) * BLOCK, :] = part[...]
    along = segments(ids, docs, (1, LENGTH), 1)
    down = segments(ids, docs, (LENGTH, 1), 0)
    logs = jnp.transpose(lse[...])
    for b in range(4):
        rows = slice(b * BLOCK, (b + 1) * BLOCK)
        same = down == along[:, rows]
        for h in range(4):
            cols = slice(h * HEAD_DIM, (h + 1) * HEAD_DIM)
            scaled = q[rows, cols] * bf16(0.125)
            scores = dot(k[:, cols], scaled, NT)
            scores = jnp.where(same, scores, -1e30)
            shares = jnp.exp(scores - logs[h : h + 1, rows])
            dots = dot(v[:, cols], g[rows, cols], NT)
            product = shares * dots
            centre = jnp.sum(product, 0, keepdims=True)
            back = (product - shares * centre).astype(bf16)
            vpart = dot(shares.astype(bf16), g[rows, cols])
            kpart = dot(back, scaled)
            if b == 0:
                vtot[:, cols] = vpart
                ktot[:, cols] = kpart
            else:
                vtot[:, cols] += vpart
                ktot[:, cols] += kpart
            dqkv[rows, cols] = (dot(back, k[:, cols], TN) * 0.125).astype(bf16)
    dqkv[:, BLOCK : 2 * BLOCK] = ktot[...].astype(bf16)
    dqkv[:, 2 * BLOCK :] = vtot[...].astype(bf16)
    sums[0:1, :] = jnp.sum(dqkv[:, :BLOCK].astype(f32), 0, keepdims=True)
    sums[1:2, :] = jnp.sum(dqkv[:, 2 * BLOCK :].astype(f32), 0, keepdims=True)
    for b, out in ((1, d1), (2, d2), (3, d3), (0, d0)):
        out[...] = dot(dqkv[b * BLOCK : (b + 1) * BLOCK, :], w[...], NT).astype(bf16)


def input_grad_kernel(ids, t0, t1, t2, t3, dqkv, own, send, made):
    core = ids[1]
    for j in range(4):
        at = lanes(ids, j)
        total = dot(t0[:, at], dqkv[:BLOCK, :], TN)
        for b, t in ((1, t1), (2, t2), (3, t3)):
            total = total + dot(t[:, at], dqkv[b * BLOCK : (b + 1) * BLOCK, :], TN)
        made[...] = total
        for out, side in ((own, core), (send, 1 - core)):
            rows = pl.ds(pl.multiple_of(side * HALF, HALF), HALF)
            for i in range(3):
                to = (j * 3 + i) * HALF
                out[to : to + HALF, :] = made[rows, i * BLOCK : (i + 1) * BLOCK].astype(bf16)


def body_for(dp, tensor):
    fast = dp == 8 and tensor == 4
    ring_pairs = [(i, (i + 1) % tensor) for i in range(tensor)]

    def flip(value, bit, axis="dp", size=dp):
        return lax.ppermute(value, axis, [(i, i ^ bit) for i in range(size)])

    def ring(value):
        return lax.ppermute(value, "tensor", ring_pairs)

    def swap(value):
        return flip(value, 1)

    def sum_all(value, over_tensor=True):
        bit = dp >> 1
        while bit:
            value = value + flip(value, bit)
            bit >>= 1
        bit = 1
        while over_tensor and bit < tensor:
            value = value + flip(value, bit, "tensor", tensor)
            bit <<= 1
        return value

    def spread(block, turn):
        by_x = flip(block, 2)
        by_y = flip(block, 4)
        far = flip(by_x, 4) if turn % 2 == 0 else flip(by_y, 2)
        return [block, by_x, by_y, far]

    def collect(parts, turn):
        own, by_x, by_y, far = parts
        if turn % 2 == 0:
            by_x = by_x + flip(far, 4)
        else:
            by_y = by_y + flip(far, 2)
        return own.astype(f32) + flip(by_x, 2).astype(f32) + flip(by_y, 4).astype(f32)

    def in_order(core, own, got, axis):
        return jnp.where(
            core == 0,
            jnp.concatenate([own, got], axis),
            jnp.concatenate([got, own], axis),
        )

    def gather_fast(core, wq, wk, wv, wo, w1, w2):
        def piece(side):
            a = lax.dynamic_slice_in_dim(w1, side * 512, 512, 1)
            b = lax.dynamic_slice_in_dim(w2, side * 512, 512, 0)
            c = lax.dynamic_slice_in_dim(wo, side * HALF, HALF, 0)
            return a, b, c

        a, b, c = piece(1 - core)
        got = swap(jnp.concatenate([a[:, i * HALF : (i + 1) * HALF] for i in range(4)] + [b, c], 0))
        a, b, c = piece(core)
        ga = jnp.concatenate([got[i * HALF : (i + 1) * HALF] for i in range(4)], 1)
        a = in_order(core, a, ga, 0)
        b = in_order(core, b, got[512:1024], 1)
        c = in_order(core, c, got[1024:], 1)
        block = jnp.concatenate([a[:, :BLOCK], a[:, BLOCK:], b, c], 0)
        first = jnp.concatenate([block, wq, wk, wv], 0)
        blocks = spread(first, 0)
        for turn in range(1, 4):
            block = ring(block)
            blocks = blocks + spread(block, turn)
        return blocks

    def gather_any(core, z, wq, wk, wv, wo, w1, w2):
        def whole(value, dim):
            value = lax.all_gather(value, "dp", axis=dim, tiled=True)
            return value

        def quarters(value):
            value = lax.all_gather(value, "tensor", axis=0, tiled=False)
            return jnp.take(value, (z - jnp.arange(tensor)) % tensor, axis=0)

        a = quarters(lax.dynamic_slice_in_dim(whole(w1, 0), core * 512, 512, 1))
        b = quarters(lax.dynamic_slice_in_dim(whole(w2, 1), core * 512, 512, 0))
        c = quarters(lax.dynamic_slice_in_dim(whole(wo, 1), core * HALF, HALF, 0))
        qkv = jnp.stack([whole(wq, 0), whole(wk, 0), whole(wv, 0)])
        qkv = qkv.reshape(3, 4, 2, HALF, BLOCK).transpose(2, 1, 0, 3, 4).reshape(2, 1536, BLOCK)
        blocks = []
        for k in range(4):
            for j in range(4):
                span = slice(j * BLOCK, (j + 1) * BLOCK)
                blocks.append(
                    jnp.concatenate(
                        [a[k, span, :BLOCK], a[k, span, BLOCK:], b[k][:, span], c[k][:, span]], 0
                    )
                )
        return blocks, qkv[core], qkv[1 - core]

    def body(
        tokens,
        cotangent,
        doc_lengths,
        query_weight,
        key_weight,
        value_weight,
        output_weight,
        inner_weight,
        outer_weight,
        query_offset,
        value_offset,
        inner_offset,
        output_offset,
        outer_offset,
        first_gain,
        first_shift,
        second_gain,
        second_shift,
    ):
        place = lax.axis_index("dp")
        z = lax.axis_index("tensor")
        core = place & 1
        chip = (place >> 1) if fast else jnp.zeros_like(place)
        ids = jnp.stack([chip, core, z]).astype(jnp.int32)
        rows = tokens.shape[0]
        width = tokens.shape[1]

        six = jnp.stack(
            [output_offset, outer_offset, first_gain, first_shift, second_gain, second_shift]
        ).astype(f32)
        piece = six.shape[1]
        six = jnp.where(
            jnp.arange(width) // piece == place * tensor + z, jnp.tile(six, (1, width // piece)), 0
        )
        two = jnp.stack([query_offset, value_offset]).astype(f32)
        piece = two.shape[1]
        two = jnp.where(
            jnp.arange(width) // piece == z * dp + place, jnp.tile(two, (1, width // piece)), 0
        )
        piece = inner_offset.shape[0]
        wide = piece * dp * tensor
        one = jnp.where(
            jnp.arange(wide) // piece == z * dp + place,
            jnp.tile(inner_offset.astype(f32), wide // piece),
            0,
        ).reshape(4, width)
        vectors = sum_all(jnp.concatenate([six, two, one], 0))
        six = [vectors[i : i + 1] for i in range(6)]
        output_bias, outer_bias, gain_one, shift_one, gain_two, shift_two = six
        query_bias = lax.dynamic_slice(vectors, (6, z * BLOCK), (1, BLOCK))
        value_bias = lax.dynamic_slice(vectors, (7, z * BLOCK), (1, BLOCK))
        inner_bias = vectors[8:12].reshape(8, 512)

        t = [tokens]
        weights = (query_weight, key_weight, value_weight, output_weight, inner_weight, outer_weight)
        if fast:
            blocks = gather_fast(core, *weights)
            own_in = jnp.concatenate([blocks[j][1152:1536] for j in range(4)], 0)
            other_in = swap(own_in)
        else:
            blocks, own_in, other_in = gather_any(core, z, *weights)
        for _ in range(3):
            t.append(ring(t[-1]))

        square = shape((LENGTH, BLOCK), bf16)
        tile = shape((BLOCK, BLOCK), bf16)
        q, k, v, w_in, m0, m1, m2, m3, lse = call(
            attend_kernel,
            "attend",
            (ids, doc_lengths, *t, own_in, other_in, query_bias, value_bias),
            [SMEM, SMEM] + [VMEM] * 8,
            [square] * 3
            + [shape((width, 3 * BLOCK), bf16)]
            + [tile] * 4
            + [shape((LENGTH, HALF), f32)],
            flops=6 << 30,
        )

        def shift(value, by):
            return lax.ppermute(value, "tensor", [(i, (i - by) % tensor) for i in range(tensor)])

        x = [m0, shift(m3, 3), shift(m2, 2), shift(m1, 1)]
        other_out = swap(jnp.concatenate([b[1024:1152] for b in blocks], 0))
        part = pl.BlockSpec((HALF, BLOCK), lambda i: (8, 0))
        wide_f = shape((rows, width), f32)
        wide_b = shape((rows, width), bf16)
        w_out, normed1, scale1, hidden_low = call(
            project_kernel,
            "project",
            (ids, tokens, *x, *blocks, other_out, output_bias, gain_one, shift_one),
            [SMEM] + [VMEM] * 5 + [part] * 16 + [VMEM] * 4,
            [shape((width, width), bf16), wide_f, shape((rows, HALF), f32), wide_b],
            flops=1 << 29,
            grid=(1,),
        )
        hidden_other = swap(hidden_low)
        tall = shape((2048, 512), bf16)
        held = [pltpu.VMEM((16, 1024, BLOCK), bf16), pltpu.VMEM((2 * rows, width), bf16)]
        active, slope, out_own, out_send = call(
            forward_kernel,
            "forward",
            (ids, hidden_low, hidden_other, inner_bias, *blocks),
            [SMEM] + [VMEM] * 3 + [HBM] * 16,
            [tall, tall, wide_f, wide_f],
            flops=4 << 30,
            scratch=held + [pltpu.SemaphoreType.DMA((16,))],
        )
        result, second_grad, second_low, second_sums = call(
            second_kernel,
            "second",
            (
                normed1,
                gain_one,
                shift_one,
                out_own,
                swap(out_send),
                outer_bias,
                gain_two,
                shift_two,
                cotangent,
            ),
            [VMEM] * 9,
            [wide_b, wide_f, wide_b, shape((3, width), f32)],
            flops=1 << 24,
        )
        second_other = swap(second_low)
        back, grad_own, grad_send, inner_sums = call(
            backward_kernel,
            "backward",
            (ids, second_low, second_other, slope, *blocks),
            [SMEM] + [VMEM] * 3 + [HBM] * 16,
            [tall, wide_f, wide_b, shape((8, 512), f32)],
            flops=4 << 30,
            scratch=held
            + [pltpu.VMEM((2 * rows, width), f32), pltpu.SemaphoreType.DMA((16,))],
        )

        def weights_of(turn):
            at = pl.BlockSpec((512, 512), lambda i: (turn, 0))
            return call(
                weights_kernel,
                "weights",
                (ids, active, back, hidden_low, hidden_other, second_low, second_other),
                [SMEM, at, at] + [VMEM] * 4,
                [shape((1024, BLOCK), bf16)] * 4,
                flops=2 << 30,
                grid=(1,),
            )

        grads = {turn: weights_of(turn) for turn in (1, 2, 3, 0)}
        first_grad, first_low, g0, g1, g2, g3, first_sums = call(
            first_kernel,
            "first",
            (second_grad, grad_own, swap(grad_send), normed1, scale1, gain_one, w_out),
            [VMEM] * 7,
            [wide_f, wide_b] + [tile] * 4 + [shape((3, width), f32)],
            flops=1 << 29,
        )
        g = [g0, shift(g3, 3), shift(g2, 2), shift(g1, 1)]
        out_part = shape((2048, BLOCK), bf16)
        wo_own, wo_send = call(
            output_grad_kernel,
            "output_grad",
            (ids, *x, first_low),
            [SMEM] + [VMEM] * 5,
            [out_part, out_part],
            flops=1 << 29,
            scratch=[pltpu.VMEM((BLOCK, width), f32)],
        )
        d0, d1, d2, d3, dqkv, head_sums = call(
            attend_back_kernel,
            "attend_back",
            (ids, doc_lengths, q, k, v, lse, *g, w_in),
            [SMEM, SMEM] + [VMEM] * 9,
            [wide_b] * 4 + [shape((LENGTH, 3 * BLOCK), bf16), shape((2, BLOCK), f32)],
            flops=12 << 30,
            scratch=[
                pltpu.VMEM((LENGTH, BLOCK), bf16),
                pltpu.VMEM((LENGTH, BLOCK), f32),
                pltpu.VMEM((LENGTH, BLOCK), f32),
            ],
        )
        in_part = shape((1536, BLOCK), bf16)
        in_own, in_send = call(
            input_grad_kernel,
            "input_grad",
            (ids, *t, dqkv),
            [SMEM] + [VMEM] * 5,
            [in_part, in_part],
            flops=2 << 30,
            scratch=[pltpu.VMEM((BLOCK, 3 * BLOCK), f32)],
        )

        moving = ring(d1)
        moving = ring((moving.astype(f32) + d2.astype(f32)).astype(bf16))
        moving = ring((moving.astype(f32) + d3.astype(f32)).astype(bf16))
        tokens_grad = first_grad + (moving.astype(f32) + d0.astype(f32))

        if fast:
            def around(parts):
                moving = ring(parts[1].astype(bf16))
                moving = ring((parts[2] + moving.astype(f32)).astype(bf16))
                moving = ring((parts[3] + moving.astype(f32)).astype(bf16))
                return parts[0] + moving.astype(f32)

            parts = {turn: collect(grads[turn], turn) for turn in (1, 2, 3, 0)}
            mine = around(parts)
            left = mine[:512].reshape(2, 2, HALF, BLOCK)
            right = mine[512:]

            def sides(side):
                a = lax.dynamic_index_in_dim(left, side, 1, False)
                b = lax.dynamic_slice_in_dim(right, side * HALF, HALF, 1)
                return a, b

            a, b = sides(1 - core)
            got = swap(
                jnp.concatenate(
                    [a[0, :, :HALF], a[0, :, HALF:], a[1, :, :HALF], a[1, :, HALF:], b], 0
                ).astype(bf16)
            ).astype(f32)
            a, b = sides(core)
            ga = jnp.concatenate([got[i * HALF : (i + 1) * HALF] for i in range(4)], 1)
            inner_grad = in_order(core, jnp.concatenate([a[0], a[1]], 1), ga, 1)
            outer_grad = in_order(core, b, got[512:], 0)

            total = (wo_own.astype(f32) + swap(wo_send).astype(f32)).astype(bf16)
            total = collect([total[j * 512 : (j + 1) * 512] for j in range(4)], 0)
            total = around([total[i * HALF : (i + 1) * HALF] for i in range(4)])
            got = swap(lax.dynamic_slice_in_dim(total, (1 - core) * HALF, HALF, 1))
            total = lax.dynamic_slice_in_dim(total, core * HALF, HALF, 1)
            output_grad = in_order(core, total, got, 0)

            total = (in_own.astype(f32) + swap(in_send).astype(f32)).astype(bf16)
            total = collect([total[j * 384 : (j + 1) * 384] for j in range(4)], 1)
            query_grad, key_grad, value_grad = [
                total[i * HALF : (i + 1) * HALF] for i in range(3)
            ]
        else:
            def scatter(value, dim):
                return lax.psum_scatter(value, "dp", scatter_dimension=dim, tiled=True)

            def quarter(parts):
                found = jnp.stack(parts).astype(f32)
                found = jnp.take(found, (z - jnp.arange(tensor)) % tensor, axis=0)
                return lax.psum_scatter(found, "tensor", scatter_dimension=0, tiled=False)

            def half(value, dim):
                field = jnp.zeros_like(value)
                return jnp.where(
                    core == 0,
                    jnp.concatenate([value, field], dim),
                    jnp.concatenate([field, value], dim),
                )

            a = quarter(
                [
                    jnp.concatenate(
                        [jnp.concatenate([p[:BLOCK], p[BLOCK:512]], 1) for p in grads[turn]], 0
                    )
                    for turn in range(4)
                ]
            )
            b = quarter(
                [jnp.concatenate([p[512:1024] for p in grads[turn]], 1) for turn in range(4)]
            )
            inner_grad = scatter(half(a, 1), 0)
            outer_grad = scatter(half(b, 0), 1)

            def heads(value):
                return value.reshape(4, 4, HALF, BLOCK).transpose(1, 2, 0, 3).reshape(4, HALF, width)

            mine, theirs = quarter(list(heads(wo_own))), quarter(list(heads(wo_send)))
            output_grad = scatter(in_order(core, mine, theirs, 0), 1)
            own, send = [p.astype(f32).reshape(4, 3, HALF, BLOCK) for p in (in_own, in_send)]
            both = jnp.where(core == 0, jnp.stack([own, send], 1), jnp.stack([send, own], 1))
            both = both.transpose(2, 0, 1, 3, 4).reshape(3, width, BLOCK)
            query_grad, key_grad, value_grad = [scatter(both[i], 0) for i in range(3)]

        sums = sum_all(jnp.concatenate([first_sums, second_sums, inner_sums.reshape(4, width)], 0))
        head_sums = sum_all(head_sums, False)
        six = lax.dynamic_slice_in_dim(sums[:6], (place * tensor + z) * (width // dp // tensor), width // dp // tensor, 1)
        offset_inner = lax.dynamic_slice_in_dim(
            sums[6:].reshape(-1), (z * dp + place) * inner_offset.shape[0], inner_offset.shape[0], 0
        )
        head_sums = lax.dynamic_slice_in_dim(head_sums, place * (BLOCK // dp), BLOCK // dp, 1)
        return (
            result,
            tokens_grad,
            query_grad,
            key_grad,
            value_grad,
            output_grad,
            inner_grad,
            outer_grad,
            head_sums[0],
            head_sums[1],
            offset_inner,
            six[0],
            six[3],
            six[1],
            six[2],
            six[4],
            six[5],
        )

    return body


def solution(mesh):
    return jax.shard_map(
        body_for(mesh.shape["dp"], mesh.shape["tensor"]),
        mesh=mesh,
        in_specs=(
            P(("dp", "tensor"), None),
            P(("dp", "tensor"), None),
            P("dp", None),
            P("dp", "tensor"),
            P("dp", "tensor"),
            P("dp", "tensor"),
            P("tensor", "dp"),
            P("dp", "tensor"),
            P("tensor", "dp"),
            P(("tensor", "dp")),
            P(("tensor", "dp")),
            P(("tensor", "dp")),
            P(("dp", "tensor")),
            P(("dp", "tensor")),
            P(("dp", "tensor")),
            P(("dp", "tensor")),
            P(("dp", "tensor")),
            P(("dp", "tensor")),
        ),
        out_specs=(
            P(("dp", "tensor"), None),
            P(("dp", "tensor"), None),
            P("dp", "tensor"),
            P("dp", "tensor"),
            P("dp", "tensor"),
            P("tensor", "dp"),
            P("dp", "tensor"),
            P("tensor", "dp"),
            P(("tensor", "dp")),
            P(("tensor", "dp")),
            P(("tensor", "dp")),
            P(("dp", "tensor")),
            P(("dp", "tensor")),
            P(("dp", "tensor")),
            P(("dp", "tensor")),
            P(("dp", "tensor")),
            P(("dp", "tensor")),
        ),
        check_vma=False,
    )
```

```python
import functools

import jax
import jax.numpy as jnp
from jax import lax
from jax.experimental import pallas as pl
from jax.experimental.pallas import tpu as pltpu
from jax.sharding import PartitionSpec as P

HEAD_DIM = 64
LENGTH = 1024
QUARTERS = 4
BLOCK = 256
HALF = 128
bf16 = jnp.bfloat16
f32 = jnp.float32
VMEM = pl.BlockSpec(memory_space=pltpu.VMEM)
SMEM = pl.BlockSpec(memory_space=pltpu.SMEM)
HBM = pl.BlockSpec(memory_space=pl.ANY)


RATE = 4e9
SPAN = {
    "prepare": 0.7,
    "assemble": 2.5,
    "pack_in": 2.5,
    "attend": 15.0,
    "pack_out": 1.6,
    "vectors": 1.6,
    "project": 5.0,
    "forward": 8.0,
    "second": 4.0,
    "backward": 10.5,
    "weights": 5.6,
    "first": 4.6,
    "output_grad": 2.9,
    "attend_back": 10.7,
    "token_grad": 5.0,
    "input_grad": 5.0,
}


def shape(dims, dtype):
    return jax.ShapeDtypeStruct(dims, dtype)


def call(kernel, name, operands, specs, outs, scratch=(), grid=()):
    return pl.pallas_call(
        kernel,
        grid=grid,
        name=name,
        out_shape=outs,
        in_specs=specs,
        out_specs=[VMEM] * len(outs),
        scratch_shapes=list(scratch),
        compiler_params=pltpu.CompilerParams(vmem_limit_bytes=26 << 20),
        cost_estimate=pl.CostEstimate(
            flops=int(SPAN[name] * RATE), bytes_accessed=0, transcendentals=0
        ),
    )(*operands)


def dot(left, right, dims=((1,), (0,))):
    return lax.dot_general(left, right, (dims, ((), ())), preferred_element_type=f32)


NT = ((1,), (1,))
TN = ((0,), (0,))


def norm_back(grad, normed, scale, gain):
    scaled = grad * gain
    return scale * (
        scaled
        - jnp.mean(scaled, -1, keepdims=True)
        - normed * jnp.mean(scaled * normed, -1, keepdims=True)
    )


def lanes(ids, j):
    return pl.ds(pl.multiple_of((ids[0] ^ j) * BLOCK, BLOCK), BLOCK)


def segments(ids, docs, dims, axis):
    place = lax.broadcasted_iota(jnp.int32, dims, axis)
    place = ((ids[2] - (place >> 8) + QUARTERS) & (QUARTERS - 1)) * BLOCK + (place & (BLOCK - 1))
    bound = docs[0, 0]
    total = (place >= bound).astype(jnp.int32)
    for j in range(1, 8):
        bound = bound + docs[0, j]
        total = total + (place >= bound).astype(jnp.int32)
    return total


SPLIT = (896, 512, 512, 512)


def find(blocks, k, j, row):
    cut = SPLIT[k]
    if j < 3:
        return blocks[k * 5 + j], row
    return (blocks[k * 5 + 3], row) if row < cut else (blocks[k * 5 + 4], row - cut)


def place_w1(k):
    return k, 0


def place_w2(k):
    return k, SPLIT[k]


def place_wo(k):
    return {0: (0, 1408), 1: (1, 1024), 2: (2, 1024), 3: (0, 1536)}[k]


def place_vectors(k):
    return {0: (0, 1664), 1: (1, 1152), 2: (2, 1152), 3: (0, 1696)}[k]


def prepare_kernel(ids, six, two, inner, wo, out):
    out[:BLOCK, :] = wo[...]
    out[BLOCK:, :] = jnp.zeros((32, HALF), bf16)
    size = six.shape[1]
    row = lax.broadcasted_iota(jnp.int32, (size, HALF), 0)
    col = lax.broadcasted_iota(jnp.int32, (size, HALF), 1)
    here = (col == row + ids[2] * size).astype(bf16)
    out[BLOCK : BLOCK + 6, :] = dot(six[...], here).astype(bf16)
    for half in range(2):
        here = (col + half * HALF == row + ids[3] * size).astype(bf16)
        at = BLOCK + half * 16
        out[at + 6 : at + 8, :] = dot(two[...], here).astype(bf16)
    out[BLOCK + 8 : BLOCK + 9, :] = inner[...]


def assemble_kernel(ids, w1, r1, w2, r2, p, rp, pb, rpb, wq, wk, wv, first, block, sems):
    core = ids[1]
    copies = []

    def put(source, out, rows, size, cols=None):
        to = out.at[pl.ds(rows, size)] if cols is None else out.at[pl.ds(rows, size), cols]
        copies.append(pltpu.make_async_copy(source, to, sems.at[len(copies)]))

    for side, v1, v2, v, vb in ((core, w1, w2, p, pb), (1 - core, r1, r2, rp, rpb)):
        cols = pl.ds(pl.multiple_of(side * HALF, HALF), HALF)
        wide = pl.ds(pl.multiple_of(core * 512, 512), 512)
        deep = pl.ds(pl.multiple_of(core * HALF, HALF), HALF)
        for out, w2_at, wo_at, vec_at in ((first, 896, 1408, 1664), (block, 512, 1024, 1152)):
            for half in range(2):
                from_cols = pl.ds(pl.multiple_of(core * 512 + half * BLOCK, BLOCK), BLOCK)
                at = pl.multiple_of(half * BLOCK + side * HALF, HALF)
                put(v1.at[:, from_cols], out, at, HALF)
                piece = v.at[pl.ds(BLOCK + half * 16, 16)]
                at = pl.multiple_of(vec_at + side * 16, 16)
                put(piece, out, at, 16, pl.ds(half * HALF, HALF))
            put(v2.at[wide], out, w2_at, 512, cols)
            put(v.at[deep], out, wo_at, HALF, cols)
        put(vb.at[deep], first, 1536, HALF, cols)
        for half in range(2):
            piece = vb.at[pl.ds(BLOCK + half * 16, 16)]
            at = pl.multiple_of(1696 + side * 16, 16)
            put(piece, first, at, 16, pl.ds(half * HALF, HALF))
    for i, piece in enumerate((wq, wk, wv)):
        put(piece, first, 512 + i * HALF, HALF)
    for copy in copies:
        copy.start()
    for copy in copies:
        copy.wait()


def pack_in_kernel(p0, p1, p2, p3, v3, out, bias):
    total = jnp.zeros((2, BLOCK), f32)
    for j, part in enumerate((p0, p1, p2, p3)):
        out[j * 384 : (j + 1) * 384, :] = part[512:896, :]
        source, row = (part, 1664) if j < 3 else (v3, 1664 - 896)
        for side in range(2):
            vectors = source[row + side * 16 : row + side * 16 + 16, :].astype(f32)
            total = total + vectors[6:8, :]
    bias[...] = total


def pack_out_kernel(turns, count, *refs):
    blocks, out, sems = refs[:count], refs[count], refs[count + 1]
    copies = []
    for n, k in enumerate(turns):
        turn, row = place_wo(k)
        for j in range(4):
            ref, row_in = find(blocks, turn, j, row)
            i = n * 4 + j
            copies.append(
                pltpu.make_async_copy(
                    ref.at[pl.ds(row_in, HALF)], out.at[pl.ds(i * HALF, HALF)], sems.at[i]
                )
            )
    for copy in copies:
        copy.start()
    for copy in copies:
        copy.wait()


def vectors_kernel(ids, *refs):
    blocks = refs[:15]
    six, inner, held, sems = refs[15:]
    copies = []
    for k in range(4):
        turn, row = place_vectors(k)
        for j in range(4):
            ref, row_in = find(blocks, turn, j, row)
            i = k * 4 + j
            copies.append(
                pltpu.make_async_copy(
                    ref.at[pl.ds(row_in, 32)], held.at[pl.ds(i * 32, 32)], sems.at[i]
                )
            )
    for copy in copies:
        copy.start()
    inner[...] = jnp.zeros(inner.shape, f32)
    for copy in copies:
        copy.wait()
    for j in range(4):
        chip = ids[0] ^ j
        for side in range(2):
            total = jnp.zeros((8, HALF), f32)
            for k in range(4):
                row = (k * 4 + j) * 32 + side * 16
                piece = held[row : row + 16, :HALF].astype(f32)
                total = total + piece[:8, :]
                at = ((ids[2] - k + QUARTERS) & (QUARTERS - 1)) * 2 + (chip >> 1)
                lane = pl.ds(pl.multiple_of((chip & 1) * BLOCK + side * HALF, HALF), HALF)
                here = lax.broadcasted_iota(jnp.int32, (8, HALF), 0) == at
                inner[:, lane] += jnp.where(here, piece[8:9, :], 0.0)
            lane = pl.multiple_of(chip * BLOCK + side * HALF, HALF)
            six[:, pl.ds(lane, HALF)] = total


def attend_kernel(ids, docs, t0, t1, t2, t3, own, other, bias, q, k, v, w, m0, m1, m2, m3, lse):
    core = ids[1]
    for j in range(4):
        base = (ids[0] ^ j) * BLOCK
        for source, side in ((own, core), (other, 1 - core)):
            rows = pl.ds(pl.multiple_of(base + side * HALF, HALF), HALF)
            for i in range(3):
                at = (j * 3 + i) * HALF
                w[rows, i * BLOCK : (i + 1) * BLOCK] = source[at : at + HALF, :]
    for b, t in enumerate((t0, t1, t2, t3)):
        rows = slice(b * BLOCK, (b + 1) * BLOCK)
        made = dot(t[...], w[...])
        q[rows, :] = (made[:, :BLOCK] + bias[0:1, :]).astype(bf16)
        k[rows, :] = made[:, BLOCK : 2 * BLOCK].astype(bf16)
        v[rows, :] = (made[:, 2 * BLOCK :] + bias[1:2, :]).astype(bf16)
    along = segments(ids, docs, (1, LENGTH), 1)
    down = segments(ids, docs, (LENGTH, 1), 0)
    for b, mixed in enumerate((m0, m1, m2, m3)):
        rows = slice(b * BLOCK, (b + 1) * BLOCK)
        same = down[rows] == along
        for h in range(4):
            cols = slice(h * HEAD_DIM, (h + 1) * HEAD_DIM)
            scores = dot(q[rows, cols] * bf16(0.125), k[:, cols], NT)
            scores = jnp.where(same, scores, -1e30)
            top = jnp.max(scores, -1, keepdims=True)
            expo = jnp.exp(scores - top)
            total = jnp.sum(expo, -1, keepdims=True)
            shares = (expo * (1.0 / total)).astype(bf16)
            mixed[:, cols] = dot(shares, v[:, cols]).astype(bf16)
            lse[rows, h : h + 1] = top + jnp.log(total)


def project_kernel(ids, tokens, x0, x1, x2, x3, other_a, other_b, vectors, *refs):
    blocks = refs[:15]
    wo, normed, scale, low, sems = refs[15:]
    core = ids[1]
    copies = []
    for n, k in enumerate((0, 3, 1, 2)):
        turn, row = place_wo(k)
        for j in range(4):
            ref, row_in = find(blocks, turn, j, row)
            got, at = (other_a, n * 4 + j) if n < 3 else (other_b, j)
            for i, (source, start, side) in enumerate(
                ((ref, row_in, core), (got, at * HALF, 1 - core))
            ):
                rows = pl.ds(pl.multiple_of(k * BLOCK + side * HALF, HALF), HALF)
                copies.append(
                    pltpu.make_async_copy(
                        source.at[pl.ds(start, HALF)],
                        wo.at[rows, lanes(ids, j)],
                        sems.at[(n * 4 + j) * 2 + i],
                    )
                )
    for copy in copies:
        copy.start()
    total = tokens[...].astype(f32) + vectors[0:1, :]
    for copy in copies:
        copy.wait()
    for k, x in enumerate((x0, x1, x2, x3)):
        total = total + dot(x[...], wo[k * BLOCK : (k + 1) * BLOCK, :])
    centered = total - jnp.mean(total, -1, keepdims=True)
    r = lax.rsqrt(jnp.mean(centered * centered, -1, keepdims=True) + 1e-05)
    n = centered * r
    normed[...] = n
    scale[...] = jnp.broadcast_to(r, scale.shape)
    low[...] = (n * vectors[2:3, :] + vectors[3:4, :]).astype(bf16)


def w1_of(blocks, k, j, half):
    ref, row = find(blocks, k, j, half * BLOCK)
    return ref[row : row + BLOCK, :]


def w2_of(blocks, k, j):
    ref, row = find(blocks, k, j, SPLIT[k])
    return ref[row : row + 512, :]


def part_of(rows, j):
    return rows[:, j * BLOCK : (j + 1) * BLOCK]


def arrange(ids, rows, mine, theirs):
    for j in range(4):
        rows[:BLOCK, j * BLOCK : (j + 1) * BLOCK] = mine[:, lanes(ids, j)]
        rows[BLOCK:, j * BLOCK : (j + 1) * BLOCK] = theirs[:, lanes(ids, j)]


def gelu_parts(inner):
    density = jnp.exp2(inner * inner * -0.7213475204444817) * 0.3989422804014327
    base = 1.0 + 0.2316419 * jnp.abs(inner)
    t = pl.reciprocal(base, approx=True)
    t = t * (2.0 - base * t)
    tail = 1.330274429 * t - 1.821255978
    tail = tail * t + 1.781477937
    tail = tail * t - 0.356563782
    tail = (tail * t + 0.319381530) * t * density
    phi = jnp.where(inner >= 0.0, 1.0 - tail, tail)
    return inner * phi, phi + inner * density


def forward_kernel(turns, ids, mine, theirs, bias, *refs):
    count = 5 * len(turns)
    blocks, refs = (None,) * (turns[0] * 5) + refs[:count], refs[count:]
    if turns[0] == 0:
        start = None
    else:
        start, refs = refs[:2], refs[2:]
    active, slope, out_mine, out_theirs, rows, total = refs
    arrange(ids, rows, mine, theirs)
    if start is not None:
        arrange(ids, total, *start)

    def inner_of(n, half):
        k = turns[n]
        at = ((ids[2] - k + QUARTERS) & (QUARTERS - 1)) * 2 + ids[1]
        offset = bias[pl.ds(at, 1), half * BLOCK : (half + 1) * BLOCK]
        total = dot(part_of(rows, 0), w1_of(blocks, k, 0, half)) + offset
        for j in range(1, 4):
            total = total + dot(part_of(rows, j), w1_of(blocks, k, j, half))
        return total

    steps = [(n, half) for n in range(len(turns)) for half in range(2)]
    inner = inner_of(*steps[0])
    for i, (n, half) in enumerate(steps):
        later = inner_of(*steps[i + 1]) if i + 1 < len(steps) else None
        span = slice(half * BLOCK, (half + 1) * BLOCK)
        deep = slice(n * 512, (n + 1) * 512)
        made, grown = gelu_parts(inner)
        active[deep, span] = made.astype(bf16)
        slope[deep, span] = grown.astype(bf16)
        if half == 1:
            for j in range(4):
                part = dot(active[deep, :], w2_of(blocks, turns[n], j))
                if n == 0 and start is None:
                    total[:, j * BLOCK : (j + 1) * BLOCK] = part
                else:
                    total[:, j * BLOCK : (j + 1) * BLOCK] += part
        inner = later
    for j in range(4):
        span = slice(j * BLOCK, (j + 1) * BLOCK)
        out_mine[:, lanes(ids, j)] = total[:BLOCK, span]
        out_theirs[:, lanes(ids, j)] = total[BLOCK:, span]


def second_kernel(normed, mine, got, vectors, cot, out, grad, low, sums):
    gain, shift = vectors[4:5, :], vectors[5:6, :]
    total = normed[...] * vectors[2:3, :] + vectors[3:4, :] + (mine[...] + got[...])
    total = total + vectors[1:2, :]
    centered = total - jnp.mean(total, -1, keepdims=True)
    r = lax.rsqrt(jnp.mean(centered * centered, -1, keepdims=True) + 1e-05)
    n = centered * r
    out[...] = (n * gain + shift).astype(bf16)
    up = cot[...].astype(f32)
    back = norm_back(up, n, r, gain)
    grad[...] = back
    low[...] = back.astype(bf16)
    sums[0:1, :] = jnp.sum(back, 0, keepdims=True)
    sums[1:2, :] = jnp.sum(up * n, 0, keepdims=True)
    sums[2:3, :] = jnp.sum(up, 0, keepdims=True)


def backward_kernel(ids, mine, theirs, slope0, slope1, *refs):
    blocks = refs[:20]
    back, out_mine, out_theirs, sums, rows, total = refs[20:]
    arrange(ids, rows, mine, theirs)
    sums[...] = jnp.zeros(sums.shape, f32)
    for k in range(4):
        span = slice(k * 512, (k + 1) * 512)
        made = dot(part_of(rows, 0), w2_of(blocks, k, 0), NT)
        for j in range(1, 4):
            made = made + dot(part_of(rows, j), w2_of(blocks, k, j), NT)
        grown = slope0[span, :] if k < 3 else slope1[...]
        made = (made * grown.astype(f32)).astype(bf16)
        back[span, :] = made
        at = ((ids[2] - k + QUARTERS) & (QUARTERS - 1)) * 2 + ids[1]
        sums[pl.ds(at, 1), :] = jnp.sum(made.astype(f32), 0, keepdims=True)
        for j in range(4):
            part = dot(made[:, :BLOCK], w1_of(blocks, k, j, 0), NT)
            part = part + dot(made[:, BLOCK:], w1_of(blocks, k, j, 1), NT)
            if k == 0:
                total[:, j * BLOCK : (j + 1) * BLOCK] = part
            else:
                total[:, j * BLOCK : (j + 1) * BLOCK] += part
    for j in range(4):
        span = slice(j * BLOCK, (j + 1) * BLOCK)
        out_mine[:, lanes(ids, j)] = total[:BLOCK, span]
        out_theirs[:, lanes(ids, j)] = total[BLOCK:, span].astype(bf16)


def weights_kernel(ids, active1, back1, active2, back2, mine, theirs, gmine, gtheirs, *outs):
    for j in range(4):
        at = lanes(ids, j)
        for active, back, out in ((active1, back1, outs[j]), (active2, back2, outs[4 + j])):
            left = dot(mine[:, at], back[:BLOCK, :], TN) + dot(theirs[:, at], back[BLOCK:, :], TN)
            out[:BLOCK, :] = left[:, :BLOCK].astype(bf16)
            out[BLOCK:512, :] = left[:, BLOCK:].astype(bf16)
            out[512:1024, :] = (
                dot(active[:BLOCK, :], gmine[:, at], TN)
                + dot(active[BLOCK:, :], gtheirs[:, at], TN)
            ).astype(bf16)


def first_kernel(second, mine, got, normed, scale, vectors, wo, grad, low, g0, g1, g2, g3, sums):
    hidden = second[...] + mine[...] + got[...].astype(f32)
    n = normed[...]
    back = norm_back(hidden, n, scale[:, :1], vectors[2:3, :])
    grad[...] = back
    rounded = back.astype(bf16)
    low[...] = rounded
    for k, g in enumerate((g0, g1, g2, g3)):
        g[...] = dot(rounded, wo[k * BLOCK : (k + 1) * BLOCK, :], NT).astype(bf16)
    sums[0:1, :] = jnp.sum(back, 0, keepdims=True)
    sums[1:2, :] = jnp.sum(hidden * n, 0, keepdims=True)
    sums[2:3, :] = jnp.sum(hidden, 0, keepdims=True)


def output_grad_kernel(ids, x0, x1, x2, x3, low, first, second, inner, own, send, made):
    core = ids[1]
    sums = jnp.concatenate([first[...], second[...], jnp.zeros((2, first.shape[1]), f32)], 0)
    for k, x in enumerate((x0, x1, x2, x3)):
        made[...] = dot(x[...], low[...], TN)
        for out, side in ((own, core), (send, 1 - core)):
            rows = pl.ds(pl.multiple_of(side * HALF, HALF), HALF)
            for j in range(4):
                at = j * 576 + k * 144
                out[at : at + HALF, :] = made[rows, lanes(ids, j)].astype(bf16)
    made[0:8, :] = sums
    for j in range(4):
        chip = ids[0] ^ j
        there = ((chip >> 1) == core).astype(f32)
        for k in range(4):
            at = ((ids[2] - k + QUARTERS) & (QUARTERS - 1)) * 2 + core
            row = inner[pl.ds(at, 1), :]
            row = jnp.where((chip & 1) == 0, row[:, :BLOCK], row[:, BLOCK:]) * there
            six = made[0:8, lanes(ids, j)]
            here = lax.broadcasted_iota(jnp.int32, (8, BLOCK), 0) == 6
            piece = jnp.concatenate([jnp.where(here, row, six), jnp.zeros((8, BLOCK), f32)], 0)
            at = j * 576 + k * 144 + HALF
            own[at : at + 16, :] = piece.astype(bf16)
            send[at : at + 16, :] = jnp.zeros((16, BLOCK), bf16)


def attend_back_kernel(heads, ids, docs, q, k, v, lse, g0, g1, g2, g3, out, sums, g, ktot, vtot):
    for b, part in enumerate((g0, g1, g2, g3)):
        g[b * BLOCK : (b + 1) * BLOCK, :] = part[...]
    along = segments(ids, docs, (1, LENGTH), 1)
    down = segments(ids, docs, (LENGTH, 1), 0)
    logs = jnp.transpose(lse[...])
    size = len(heads) * HEAD_DIM
    for b in range(4):
        rows = slice(b * BLOCK, (b + 1) * BLOCK)
        same = down == along[:, rows]
        for n, h in enumerate(heads):
            cols = slice(h * HEAD_DIM, (h + 1) * HEAD_DIM)
            to = slice(n * HEAD_DIM, (n + 1) * HEAD_DIM)
            scaled = q[rows, cols] * bf16(0.125)
            scores = dot(k[:, cols], scaled, NT)
            scores = jnp.where(same, scores, -1e30)
            shares = jnp.exp(scores - logs[h : h + 1, rows])
            dots = dot(v[:, cols], g[rows, cols], NT)
            product = shares * dots
            centre = jnp.sum(product, 0, keepdims=True)
            back = (product - shares * centre).astype(bf16)
            vpart = dot(shares.astype(bf16), g[rows, cols])
            kpart = dot(back, scaled)
            if b == 0:
                vtot[:, to] = vpart
                ktot[:, to] = kpart
            else:
                vtot[:, to] += vpart
                ktot[:, to] += kpart
            out[rows, to] = (dot(back, k[:, cols], TN) * 0.125).astype(bf16)
    out[:, size : 2 * size] = ktot[...].astype(bf16)
    out[:, 2 * size :] = vtot[...].astype(bf16)
    sums[0:1, :] = jnp.sum(out[:, :size].astype(f32), 0, keepdims=True)
    sums[1:2, :] = jnp.sum(out[:, 2 * size :].astype(f32), 0, keepdims=True)


def token_grad_kernel(low, high, w, wo, d0, d1, d2, d3, dqkv):
    for part, at in ((low, 0), (high, HALF)):
        for i in range(3):
            dqkv[:, i * BLOCK + at : i * BLOCK + at + HALF] = part[:, i * HALF : (i + 1) * HALF]
    for b, out in ((1, d1), (2, d2), (3, d3), (0, d0)):
        rows = slice(b * BLOCK, (b + 1) * BLOCK)
        out[:BLOCK, :] = dot(dqkv[rows, :], w[...], NT).astype(bf16)
        for i in range(3):
            at = b * 144 + i * 48
            out[BLOCK:, i * BLOCK : (i + 1) * BLOCK] = wo[at : at + 48, :]
        out[BLOCK:, 3 * BLOCK :] = jnp.zeros((48, BLOCK), bf16)


def input_grad_kernel(ids, t0, t1, t2, t3, dqkv, sums, own, send, made):
    core = ids[1]
    vectors = jnp.concatenate([sums[...], jnp.zeros((14, BLOCK), f32)], 0).astype(bf16)
    for j in range(4):
        for out in (own, send):
            out[j * 400 + 384 : (j + 1) * 400, :] = vectors
    for j in range(4):
        at = lanes(ids, j)
        total = dot(t0[:, at], dqkv[:BLOCK, :], TN)
        for b, t in ((1, t1), (2, t2), (3, t3)):
            total = total + dot(t[:, at], dqkv[b * BLOCK : (b + 1) * BLOCK, :], TN)
        made[...] = total
        for out, side in ((own, core), (send, 1 - core)):
            rows = pl.ds(pl.multiple_of(side * HALF, HALF), HALF)
            for i in range(3):
                to = j * 400 + i * HALF
                out[to : to + HALF, :] = made[rows, i * BLOCK : (i + 1) * BLOCK].astype(bf16)


def body_for(dp, tensor):
    fast = dp == 8 and tensor == 4
    ring_pairs = [(i, (i + 1) % tensor) for i in range(tensor)]

    def flip(value, bit, axis="dp", size=dp):
        return lax.ppermute(value, axis, [(i, i ^ bit) for i in range(size)])

    def ring(value):
        return lax.ppermute(value, "tensor", ring_pairs)

    def swap(value):
        return flip(value, 1)

    def sum_all(value, over_tensor=True):
        bit = dp >> 1
        while bit:
            value = value + flip(value, bit)
            bit >>= 1
        bit = 1
        while over_tensor and bit < tensor:
            value = value + flip(value, bit, "tensor", tensor)
            bit <<= 1
        return value

    def in_order(core, own, got, axis):
        return jnp.where(
            core == 0,
            jnp.concatenate([own, got], axis),
            jnp.concatenate([got, own], axis),
        )

    def after(value, *others):
        return lax.optimization_barrier((value, *others))[0]

    def assemble(ids, prepared, wq, wk, wv, w1, w2):
        pairs = [
            ((p * tensor + i), ((p ^ 1) * tensor + (i + tensor - 1) % tensor))
            for p in range(dp)
            for i in range(tensor)
        ]
        back = [(i, (i + tensor - 1) % tensor) for i in range(tensor)]
        ahead = lax.ppermute(prepared, "tensor", back)
        crossed = lax.ppermute(prepared, ("dp", "tensor"), pairs)
        made = call(
            assemble_kernel,
            "assemble",
            (ids, w1, swap(w1), w2, swap(w2), prepared, swap(prepared), ahead, crossed, wq, wk, wv),
            [SMEM] + [HBM] * 11,
            [shape((1728, BLOCK), bf16), shape((1184, BLOCK), bf16)],
            scratch=[pltpu.SemaphoreType.DMA((33,))],
        )
        return made, ahead

    def gather_any(core, z, wq, wk, wv, wo, w1, w2):
        def whole(value, dim):
            value = lax.all_gather(value, "dp", axis=dim, tiled=True)
            return value

        def quarters(value):
            value = lax.all_gather(value, "tensor", axis=0, tiled=False)
            return jnp.take(value, (z - jnp.arange(tensor)) % tensor, axis=0)

        a = quarters(lax.dynamic_slice_in_dim(whole(w1, 0), core * 512, 512, 1))
        b = quarters(lax.dynamic_slice_in_dim(whole(w2, 1), core * 512, 512, 0))
        c = quarters(lax.dynamic_slice_in_dim(whole(wo, 1), core * HALF, HALF, 0))
        qkv = jnp.stack([whole(wq, 0), whole(wk, 0), whole(wv, 0)])
        qkv = qkv.reshape(3, 4, 2, HALF, BLOCK).transpose(2, 1, 0, 3, 4).reshape(2, 1536, BLOCK)
        blocks = []
        for k in range(4):
            made = []
            for j in range(4):
                span = slice(j * BLOCK, (j + 1) * BLOCK)
                left = [a[k, span, :BLOCK], a[k, span, BLOCK:]]
                right = [b[k][:, span], c[k][:, span]]
                if k == 0:
                    left.append(jnp.zeros((384, BLOCK), bf16))
                    right += [c[3][:, span], jnp.zeros((64, BLOCK), bf16)]
                else:
                    right.append(jnp.zeros((32, BLOCK), bf16))
                made.append(jnp.concatenate(left + right, 0))
            blocks += made[:3] + [made[3][: SPLIT[k]], made[3][SPLIT[k] :]]
        return blocks, qkv[core], qkv[1 - core]

    def body(
        tokens,
        cotangent,
        doc_lengths,
        query_weight,
        key_weight,
        value_weight,
        output_weight,
        inner_weight,
        outer_weight,
        query_offset,
        value_offset,
        inner_offset,
        output_offset,
        outer_offset,
        first_gain,
        first_shift,
        second_gain,
        second_shift,
    ):
        place = lax.axis_index("dp")
        z = lax.axis_index("tensor")
        core = place & 1
        chip = (place >> 1) if fast else jnp.zeros_like(place)
        ids = jnp.stack([chip, core, z, place]).astype(jnp.int32)
        rows = tokens.shape[0]
        width = tokens.shape[1]

        six = jnp.stack(
            [output_offset, outer_offset, first_gain, first_shift, second_gain, second_shift]
        )
        two = jnp.stack([query_offset, value_offset])
        weights = (query_weight, key_weight, value_weight)
        t = [tokens]
        if fast:
            prepared = call(
                prepare_kernel,
                "prepare",
                (ids, six, two, inner_offset[None], output_weight),
                [SMEM] + [VMEM] * 4,
                [shape((BLOCK + 32, HALF), bf16)],
            )[0]
            (first, block), ahead = assemble(
                ids, prepared, *weights, inner_weight, outer_weight
            )
            t.append(ring(after(tokens, ahead)))

            def spread(k, own, by_x, by_y):
                cut = SPLIT[k]
                return flip(by_x[:cut], 4), flip(by_y[cut:], 2)

            x0, y0, z1 = flip(first, 2), flip(first, 4), ring(block)
            t.append(ring(t[1]))
            z1, x0, y0, t[2] = lax.optimization_barrier((z1, x0, y0, t[2]))
            x1, y1, z2 = flip(z1, 2), flip(z1, 4), ring(z1)
            a0, b0 = spread(0, first, x0, y0)
            t.append(ring(t[2]))
            z2, x1, y1, a0, b0, t[3] = lax.optimization_barrier((z2, x1, y1, a0, b0, t[3]))
            x2, y2, z3 = flip(z2, 2), flip(z2, 4), ring(z2)
            a1, b1 = spread(1, z1, x1, y1)
            own_in, qv_bias = call(
                pack_in_kernel,
                "pack_in",
                (first, x0, y0, a0, b0),
                [VMEM] * 5,
                [shape((1536, BLOCK), bf16), shape((2, BLOCK), f32)],
            )
            other_in = swap(own_in)
        else:
            piece = six.shape[1]
            field = jnp.arange(width) // piece == place * tensor + z
            six = jnp.where(field, jnp.tile(six.astype(f32), (1, width // piece)), 0)
            piece = two.shape[1]
            field = jnp.arange(width) // piece == z * dp + place
            two = jnp.where(field, jnp.tile(two.astype(f32), (1, width // piece)), 0)
            piece = inner_offset.shape[0]
            wide = piece * dp * tensor
            field = jnp.arange(wide) // piece == z * dp + place
            one = jnp.where(field, jnp.tile(inner_offset.astype(f32), wide // piece), 0)
            vectors = sum_all(jnp.concatenate([six, two, one.reshape(4, width)], 0))
            qv_bias = lax.dynamic_slice(vectors, (6, z * BLOCK), (2, BLOCK))
            inner_bias = vectors[8:12].reshape(8, 512)
            vectors = vectors[:8]
            blocks, own_in, other_in = gather_any(
                core, z, *weights, output_weight, inner_weight, outer_weight
            )
            for _ in range(3):
                t.append(ring(t[-1]))

        square = shape((LENGTH, BLOCK), bf16)
        tile = shape((BLOCK, BLOCK), bf16)
        q, k, v, w_in, m0, m1, m2, m3, lse = call(
            attend_kernel,
            "attend",
            (ids, doc_lengths, *t, own_in, other_in, qv_bias),
            [SMEM, SMEM] + [VMEM] * 7,
            [square] * 3
            + [shape((width, 3 * BLOCK), bf16)]
            + [tile] * 4
            + [shape((LENGTH, HALF), f32)],
        )

        def shift(value, by):
            return lax.ppermute(value, "tensor", [(i, (i - by) % tensor) for i in range(tensor)])

        if fast:
            z3, x2, y2, a1, b1, m0 = lax.optimization_barrier((z3, x2, y2, a1, b1, m0))
            x3, y3 = flip(z3, 2), flip(z3, 4)
            a2, b2 = spread(2, z2, x2, y2)
        x = [m0, shift(m3, 3), shift(m2, 2), shift(m1, 1)]

        def pack_out(turns, blocks):
            size = len(turns) * 4
            return swap(
                call(
                    functools.partial(pack_out_kernel, turns, len(blocks)),
                    "pack_out",
                    tuple(blocks),
                    [HBM] * len(blocks),
                    [shape((size * HALF, BLOCK), bf16)],
                    scratch=[pltpu.SemaphoreType.DMA((size,))],
                )[0]
            )

        if fast:
            blocks = [first, x0, y0, a0, b0, z1, x1, y1, a1, b1]
        other_a = pack_out((0, 3, 1), blocks[:10])
        if fast:
            x3, y3, a2, b2, *x = lax.optimization_barrier((x3, y3, a2, b2, *x))
            a3, b3 = spread(3, z3, x3, y3)
            blocks += [z2, x2, y2, a2, b2, z3, x3, y3, a3, b3]
            vectors, inner_bias = call(
                vectors_kernel,
                "vectors",
                (ids, *blocks[:15]),
                [SMEM] + [HBM] * 15,
                [shape((8, width), f32), shape((8, 512), f32)],
                scratch=[pltpu.VMEM((512, BLOCK), bf16), pltpu.SemaphoreType.DMA((16,))],
            )
        other_b = pack_out((2,), blocks[:15])
        wide_f = shape((rows, width), f32)
        wide_b = shape((rows, width), bf16)
        w_out, normed1, scale1, hidden_low = call(
            project_kernel,
            "project",
            (ids, tokens, *x, other_a, other_b, vectors, *blocks[:15]),
            [SMEM] + [VMEM] * 5 + [HBM] * 2 + [VMEM] + [HBM] * 15,
            [shape((width, width), bf16), wide_f, shape((rows, HALF), f32), wide_b],
            scratch=[pltpu.SemaphoreType.DMA((32,))],
        )
        hidden_other = swap(hidden_low)

        def forward(turns, *start):
            count = len(turns)
            tall = shape((count * 512, 512), bf16)
            return call(
                functools.partial(forward_kernel, turns),
                "forward",
                (ids, hidden_low, hidden_other, inner_bias)
                + tuple(blocks[turns[0] * 5 : turns[-1] * 5 + 5])
                + start,
                [SMEM] + [VMEM] * (3 + 5 * count + len(start)),
                [tall, tall, wide_f, wide_f],
                scratch=[
                    pltpu.VMEM((2 * rows, width), bf16),
                    pltpu.VMEM((2 * rows, width), f32),
                ],
            )

        active0, slope0, out_own, out_send = forward((0, 1, 2))
        active1, slope1, out_own, out_send = forward((3,), out_own, out_send)
        result, second_grad, second_low, second_sums = call(
            second_kernel,
            "second",
            (
                normed1,
                out_own,
                swap(out_send),
                vectors,
                cotangent,
            ),
            [VMEM] * 5,
            [wide_b, wide_f, wide_b, shape((3, width), f32)],
        )
        second_other = swap(second_low)
        tall = shape((2048, 512), bf16)
        back, grad_own, grad_send, inner_sums = call(
            backward_kernel,
            "backward",
            (ids, second_low, second_other, slope0, slope1, *blocks),
            [SMEM] + [VMEM] * 24,
            [tall, wide_f, wide_b, shape((8, 512), f32)],
            scratch=[
                pltpu.VMEM((2 * rows, width), bf16),
                pltpu.VMEM((2 * rows, width), f32),
            ],
        )

        def weights_of(turns, *others):
            def at(turn):
                return pl.BlockSpec((512, 512), lambda i: (turn, 0))

            def active_of(turn):
                return (active0, at(turn)) if turn < 3 else (active1, at(0))

            (a, a_at), (b, b_at) = active_of(turns[0]), active_of(turns[1])
            made = call(
                weights_kernel,
                "weights",
                (
                    ids,
                    a,
                    back,
                    b,
                    back,
                    hidden_low,
                    hidden_other,
                    second_low,
                    after(second_other, *others),
                ),
                [SMEM, a_at, at(turns[0]), b_at, at(turns[1])] + [VMEM] * 4,
                [shape((1024, BLOCK), bf16)] * 8,
                grid=(1,),
            )
            return {turns[0]: made[:4], turns[1]: made[4:]}

        grad_got = swap(grad_send)
        grads = weights_of((1, 2))
        first_grad, first_low, g0, g1, g2, g3, first_sums = call(
            first_kernel,
            "first",
            (
                second_grad,
                grad_own,
                after(grad_got, *grads[1]),
                normed1,
                scale1,
                vectors,
                w_out,
            ),
            [VMEM] * 7,
            [wide_f, wide_b] + [tile] * 4 + [shape((3, width), f32)],
        )
        g = [g0, shift(g3, 3), shift(g2, 2), shift(g1, 1)]
        grads.update(weights_of((3, 0), first_low))

        def meet(parts, turn):
            own, by_x, by_y, far = parts
            if turn % 2 == 0:
                return [own, by_x + flip(far, 4), by_y]
            return [own, by_x, by_y + flip(far, 2)]

        out_part = shape((2304, BLOCK), bf16)
        wo_own, wo_send = call(
            output_grad_kernel,
            "output_grad",
            (ids, *x, first_low, first_sums, second_sums, inner_sums),
            [SMEM] + [VMEM] * 8,
            [out_part, out_part],
            scratch=[pltpu.VMEM((BLOCK, width), f32)],
        )
        if fast:
            met = {turn: meet(grads[turn], turn) for turn in (1, 2)}
            wo_got = swap(wo_send)
            g[0] = after(g[0], met[1][2], met[2][1])

            def send(turn):
                return flip(met[turn][1], 2), flip(met[turn][2], 4)

            sent = {turn: send(turn) for turn in (1, 2)}

            def settle(turn, moving=None):
                total = (
                    met[turn][0].astype(f32)
                    + sent[turn][0].astype(f32)
                    + sent[turn][1].astype(f32)
                )
                return total if moving is None else total + moving.astype(f32)

        def attend_back(heads, g):
            size = len(heads) * HEAD_DIM
            return call(
                functools.partial(attend_back_kernel, heads),
                "attend_back",
                (ids, doc_lengths, q, k, v, lse, *g),
                [SMEM, SMEM] + [VMEM] * 8,
                [shape((LENGTH, 3 * size), bf16), shape((2, size), f32)],
                scratch=[
                    pltpu.VMEM((LENGTH, BLOCK), bf16),
                    pltpu.VMEM((LENGTH, size), f32),
                    pltpu.VMEM((LENGTH, size), f32),
                ],
            )

        if fast:
            wo_total = (wo_own.astype(f32) + wo_got.astype(f32)).astype(bf16)
            wo_parts = [wo_total[j * 576 : (j + 1) * 576] for j in range(4)]
            wo_far = flip(wo_parts[3], 4)
        dqkv_low, sums_low = attend_back((0, 1), g)
        if fast:
            gated = [*grads[3][1:3], *grads[0][1:3], *sent[1], wo_far, dqkv_low]
            gated = lax.optimization_barrier(tuple(gated))
            met[3] = meet([grads[3][0], *gated[0:2], grads[3][3]], 3)
            met[0] = meet([grads[0][0], *gated[2:4], grads[0][3]], 0)
            sent.update({turn: send(turn) for turn in (3, 0)})
            sent[1] = gated[4:6]
            total1 = settle(1).astype(bf16)
            moving1 = ring(total1)
            wo_x = flip(wo_parts[1] + gated[6], 2)
            wo_y = flip(wo_parts[2], 4)
            g[0] = after(g[0], dqkv_low, met[3][2], met[0][1], total1)
        dqkv_high, sums_high = attend_back((2, 3), g)
        head_sums = jnp.concatenate([sums_low, sums_high], 1)
        if fast:
            moving1, dqkv_high, wo_x, wo_y, *sent[2] = lax.optimization_barrier(
                (moving1, dqkv_high, wo_x, wo_y, *sent[2])
            )
            total2 = settle(2, moving1).astype(bf16)
            moving2 = ring(total2)
            wo_total = wo_parts[0].astype(f32) + wo_x.astype(f32) + wo_y.astype(f32)
            wo_total = after(wo_total.astype(bf16), total2)
        else:
            wo_total = wo_own[:576]
        moved = shape((rows + 48, width), bf16)
        d0, d1, d2, d3, dqkv = call(
            token_grad_kernel,
            "token_grad",
            (dqkv_low, dqkv_high, w_in, wo_total),
            [VMEM] * 4,
            [moved] * 4 + [shape((LENGTH, 3 * BLOCK), bf16)],
        )
        in_part = shape((1600, BLOCK), bf16)
        in_own, in_send = call(
            input_grad_kernel,
            "input_grad",
            (ids, *t, dqkv, head_sums),
            [SMEM] + [VMEM] * 6,
            [in_part, in_part],
            scratch=[pltpu.VMEM((BLOCK, 3 * BLOCK), f32)],
        )

        def add(left, right):
            return (left.astype(f32) + right.astype(f32)).astype(bf16)

        moving = ring(d1)
        if fast:
            in_got = swap(in_send)
            moving, moving2, in_got, *sent[3] = lax.optimization_barrier(
                (moving, moving2, in_got, *sent[3])
            )
            moving = ring(add(moving, d2))
            total3 = settle(3, moving2).astype(bf16)
            moving3 = ring(total3)
            in_total = add(in_own, in_got)
            in_parts = [in_total[j * 400 : (j + 1) * 400] for j in range(4)]
            in_far = flip(in_parts[3], 2)
            moving, moving3, in_far, *sent[0] = lax.optimization_barrier(
                (moving, moving3, in_far, *sent[0])
            )
            moving = ring(add(moving, d3))
            in_x = flip(in_parts[1], 2)
            in_y = flip(in_parts[2] + in_far, 4)
            mine = settle(0, moving3)
        else:
            moving = ring(add(moving, d2))
            moving = ring(add(moving, d3))
        moving = moving.astype(f32) + d0.astype(f32)
        tokens_grad = first_grad + moving[:rows]

        if fast:
            left = mine[:512].reshape(2, 2, HALF, BLOCK)
            right = mine[512:]

            def sides(side):
                a = lax.dynamic_index_in_dim(left, side, 1, False)
                b = lax.dynamic_slice_in_dim(right, side * HALF, HALF, 1)
                return a, b

            a, b = sides(1 - core)
            got = swap(
                jnp.concatenate(
                    [a[0, :, :HALF], a[0, :, HALF:], a[1, :, :HALF], a[1, :, HALF:], b], 0
                ).astype(bf16)
            ).astype(f32)
            a, b = sides(core)
            ga = jnp.concatenate([got[i * HALF : (i + 1) * HALF] for i in range(4)], 1)
            inner_grad = in_order(core, jnp.concatenate([a[0], a[1]], 1), ga, 1)
            outer_grad = in_order(core, b, got[512:], 0)

            total = jnp.concatenate(
                [moving[rows:, i * BLOCK : (i + 1) * BLOCK] for i in range(3)], 0
            )
            got = swap(lax.dynamic_slice_in_dim(total, (1 - core) * HALF, HALF, 1))
            total = lax.dynamic_slice_in_dim(total, core * HALF, HALF, 1)
            output_grad = in_order(core, total[:HALF], got[:HALF], 0)
            sums = total[HALF:] + got[HALF:]
            six = lax.dynamic_slice(sums, (0, z * 32), (6, 32))
            offset_inner = sums[6]

            total = in_parts[0].astype(f32) + in_x.astype(f32) + in_y.astype(f32)
            query_grad, key_grad, value_grad = [
                total[i * HALF : (i + 1) * HALF] for i in range(3)
            ]
            head_sums = total[384:386]
        else:
            def scatter(value, dim):
                return lax.psum_scatter(value, "dp", scatter_dimension=dim, tiled=True)

            def quarter(parts):
                found = jnp.stack(parts).astype(f32)
                found = jnp.take(found, (z - jnp.arange(tensor)) % tensor, axis=0)
                return lax.psum_scatter(found, "tensor", scatter_dimension=0, tiled=False)

            def half(value, dim):
                field = jnp.zeros_like(value)
                return jnp.where(
                    core == 0,
                    jnp.concatenate([value, field], dim),
                    jnp.concatenate([field, value], dim),
                )

            a = quarter(
                [
                    jnp.concatenate(
                        [jnp.concatenate([p[:BLOCK], p[BLOCK:512]], 1) for p in grads[turn]], 0
                    )
                    for turn in range(4)
                ]
            )
            b = quarter(
                [jnp.concatenate([p[512:1024] for p in grads[turn]], 1) for turn in range(4)]
            )
            inner_grad = scatter(half(a, 1), 0)
            outer_grad = scatter(half(b, 0), 1)

            def heads(value):
                value = value.reshape(4, 4, 144, BLOCK)[:, :, :HALF]
                return value.transpose(1, 2, 0, 3).reshape(4, HALF, width)

            mine, theirs = quarter(list(heads(wo_own))), quarter(list(heads(wo_send)))
            output_grad = scatter(in_order(core, mine, theirs, 0), 1)
            own, send = [
                p.astype(f32).reshape(4, 400, BLOCK)[:, :384].reshape(4, 3, HALF, BLOCK)
                for p in (in_own, in_send)
            ]
            both = jnp.where(core == 0, jnp.stack([own, send], 1), jnp.stack([send, own], 1))
            both = both.transpose(2, 0, 1, 3, 4).reshape(3, width, BLOCK)
            query_grad, key_grad, value_grad = [scatter(both[i], 0) for i in range(3)]

            sums = jnp.concatenate([first_sums, second_sums, inner_sums.reshape(4, width)], 0)
            sums = sum_all(sums)
            head_sums = sum_all(head_sums, False)
            piece = width // (dp * tensor)
            six = lax.dynamic_slice_in_dim(sums[:6], (place * tensor + z) * piece, piece, 1)
            piece = inner_offset.shape[0]
            offset_inner = lax.dynamic_slice_in_dim(
                sums[6:].reshape(-1), (z * dp + place) * piece, piece, 0
            )

        head_sums = lax.dynamic_slice_in_dim(head_sums, place * (BLOCK // dp), BLOCK // dp, 1)
        return (
            result,
            tokens_grad,
            query_grad,
            key_grad,
            value_grad,
            output_grad,
            inner_grad,
            outer_grad,
            head_sums[0],
            head_sums[1],
            offset_inner,
            six[0],
            six[3],
            six[1],
            six[2],
            six[4],
            six[5],
        )

    return body


def solution(mesh):
    return jax.shard_map(
        body_for(mesh.shape["dp"], mesh.shape["tensor"]),
        mesh=mesh,
        in_specs=(
            P(("dp", "tensor"), None),
            P(("dp", "tensor"), None),
            P("dp", None),
            P("dp", "tensor"),
            P("dp", "tensor"),
            P("dp", "tensor"),
            P("tensor", "dp"),
            P("dp", "tensor"),
            P("tensor", "dp"),
            P(("tensor", "dp")),
            P(("tensor", "dp")),
            P(("tensor", "dp")),
            P(("dp", "tensor")),
            P(("dp", "tensor")),
            P(("dp", "tensor")),
            P(("dp", "tensor")),
            P(("dp", "tensor")),
            P(("dp", "tensor")),
        ),
        out_specs=(
            P(("dp", "tensor"), None),
            P(("dp", "tensor"), None),
            P("dp", "tensor"),
            P("dp", "tensor"),
            P("dp", "tensor"),
            P("tensor", "dp"),
            P("dp", "tensor"),
            P("tensor", "dp"),
            P(("tensor", "dp")),
            P(("tensor", "dp")),
            P(("tensor", "dp")),
            P(("dp", "tensor")),
            P(("dp", "tensor")),
            P(("dp", "tensor")),
            P(("dp", "tensor")),
            P(("dp", "tensor")),
            P(("dp", "tensor")),
        ),
        check_vma=False,
    )
```

```python
import functools

import jax
import jax.numpy as jnp
from jax import lax
from jax.experimental import pallas as pl
from jax.experimental.pallas import tpu as pltpu
from jax.sharding import PartitionSpec as P

HEAD_DIM = 64
LENGTH = 1024
QUARTERS = 4
BLOCK = 256
HALF = 128
bf16 = jnp.bfloat16
f32 = jnp.float32
VMEM = pl.BlockSpec(memory_space=pltpu.VMEM)
SMEM = pl.BlockSpec(memory_space=pltpu.SMEM)
HBM = pl.BlockSpec(memory_space=pl.ANY)


RATE = 4e9
SPAN = {
    "prepare": 0.7,
    "assemble": 2.5,
    "ahead": 0.5,
    "join": 0.8,
    "pack_in": 2.5,
    "attend": 10.0,
    "pack_out": 1.6,
    "vectors": 1.6,
    "project": 5.0,
    "forward": 8.0,
    "second": 4.0,
    "backward": 10.5,
    "weights": 5.6,
    "first": 4.6,
    "output_grad": 2.9,
    "attend_back": 6.5,
    "token_grad": 0.1,
    "input_grad": 0.9,
}

ROOM = {"attend": 28, "project": 14, "forward": 26, "backward": 30, "weights": 16, "attend_back": 24}


def shape(dims, dtype):
    return jax.ShapeDtypeStruct(dims, dtype)


def call(kernel, name, operands, specs, outs, scratch=(), grid=()):
    return pl.pallas_call(
        kernel,
        grid=grid,
        name=name,
        out_shape=outs,
        in_specs=specs,
        out_specs=[VMEM] * len(outs),
        scratch_shapes=list(scratch),
        compiler_params=pltpu.CompilerParams(vmem_limit_bytes=ROOM.get(name, 12) << 20),
        cost_estimate=pl.CostEstimate(
            flops=int(SPAN[name] * RATE), bytes_accessed=0, transcendentals=0
        ),
    )(*operands)


def dot(left, right, dims=((1,), (0,))):
    return lax.dot_general(left, right, (dims, ((), ())), preferred_element_type=f32)


NT = ((1,), (1,))
TN = ((0,), (0,))


def norm_back(grad, normed, scale, gain):
    scaled = grad * gain
    return scale * (
        scaled
        - jnp.mean(scaled, -1, keepdims=True)
        - normed * jnp.mean(scaled * normed, -1, keepdims=True)
    )


def lanes(ids, j):
    return pl.ds(pl.multiple_of((ids[0] ^ j) * BLOCK, BLOCK), BLOCK)


def segments(ids, docs, dims, axis):
    place = lax.broadcasted_iota(jnp.int32, dims, axis)
    place = ((ids[2] - (place >> 8) + QUARTERS) & (QUARTERS - 1)) * BLOCK + (place & (BLOCK - 1))
    bound = docs[0, 0]
    total = (place >= bound).astype(jnp.int32)
    for j in range(1, 8):
        bound = bound + docs[0, j]
        total = total + (place >= bound).astype(jnp.int32)
    return total


SPLIT = (896, 512, 512, 512)
PLACES = (
    (("first", 0), ("x0", 0), ("y0", 0), ("y1", 1184), ("x1", 1184)),
    (("z1", 0), ("x1", 0), ("y1", 0), ("y2", 1184), ("x2", 1184)),
    (("z2", 0), ("x2", 0), ("y2", 0), ("y3", 1184), ("x3", 1184)),
    (("z3", 0), ("x3", 0), ("y3", 0), ("y4", 0), ("x4", 0)),
)
AHEAD = (("ahead", 0), ("x1", 1856), ("y1", 2080), ("y2", 1696))
EARLY = ("first", "x0", "y0", "z1", "x1", "y1", "x2", "y2", "ahead")
MIDDLE = EARLY + ("z2", "x3", "y3")
WEIGHTS = MIDDLE[:8] + MIDDLE[9:]
LAST = ("z3", "x3", "y3", "x4", "y4")
ALL = WEIGHTS + ("z3", "x4", "y4")


def find(blocks, k, j, row):
    part = j
    if j == 3 and row >= SPLIT[k]:
        part, row = 4, row - SPLIT[k]
    name, start = PLACES[k][part]
    return blocks[name], start + row


def find_ahead(blocks, k, j, row):
    if k < 3:
        return find(blocks, k, j, SPLIT[k] + 512 + row)
    name, start = AHEAD[j]
    return blocks[name], start + row


def prepare_kernel(ids, six, two, inner, wo, out):
    out[:BLOCK, :] = wo[...]
    out[BLOCK:, :] = jnp.zeros((32, HALF), bf16)
    size = six.shape[1]
    row = lax.broadcasted_iota(jnp.int32, (size, HALF), 0)
    col = lax.broadcasted_iota(jnp.int32, (size, HALF), 1)
    here = (col == row + ids[2] * size).astype(bf16)
    out[BLOCK : BLOCK + 6, :] = dot(six[...], here).astype(bf16)
    for half in range(2):
        here = (col + half * HALF == row + ids[3] * size).astype(bf16)
        at = BLOCK + half * 16
        out[at + 6 : at + 8, :] = dot(two[...], here).astype(bf16)
    out[BLOCK + 8 : BLOCK + 9, :] = inner[...]


def assemble_kernel(ids, w1, r1, w2, r2, p, rp, wq, wk, wv, tokens, first, block, sems):
    core = ids[1]
    copies = []

    def put(source, out, rows, size, cols=None):
        to = out.at[pl.ds(rows, size)] if cols is None else out.at[pl.ds(rows, size), cols]
        copies.append(pltpu.make_async_copy(source, to, sems.at[len(copies)]))

    for side, v1, v2, v in ((core, w1, w2, p), (1 - core, r1, r2, rp)):
        cols = pl.ds(pl.multiple_of(side * HALF, HALF), HALF)
        wide = pl.ds(pl.multiple_of(core * 512, 512), 512)
        for out, w2_at in ((first, 896), (block, 512)):
            for half in range(2):
                from_cols = pl.ds(pl.multiple_of(core * 512 + half * BLOCK, BLOCK), BLOCK)
                at = pl.multiple_of(half * BLOCK + side * HALF, HALF)
                put(v1.at[:, from_cols], out, at, HALF)
            put(v2.at[wide], out, w2_at, 512, cols)
            put_rest(put, core, side, v, out, w2_at + 512)
    for i, piece in enumerate((wq, wk, wv)):
        put(piece, first, 512 + i * HALF, HALF)
    for j in range(4):
        put(tokens.at[:, pl.ds(j * BLOCK, BLOCK)], block, 1184 + j * BLOCK, BLOCK)
    for copy in copies:
        copy.start()
    for copy in copies:
        copy.wait()


def join_kernel(spans, *refs):
    outs = refs[len(refs) - len(spans) :]
    for out, pieces in zip(outs, spans):
        at = 0
        for n, row, size in pieces:
            out[at : at + size, :] = refs[n][row : row + size, :]
            at += size


def put_rest(put, core, side, v, out, row):
    deep = pl.ds(pl.multiple_of(core * HALF, HALF), HALF)
    put(v.at[deep], out, row, HALF, pl.ds(pl.multiple_of(side * HALF, HALF), HALF))
    for half in range(2):
        piece = v.at[pl.ds(BLOCK + half * 16, 16)]
        at = pl.multiple_of(row + HALF + side * 16, 16)
        put(piece, out, at, 16, pl.ds(half * HALF, HALF))


def ahead_kernel(ids, p, rp, out, sems):
    core = ids[1]
    copies = []

    def put(source, out, rows, size, cols):
        to = out.at[pl.ds(rows, size), cols]
        copies.append(pltpu.make_async_copy(source, to, sems.at[len(copies)]))

    put_rest(put, core, core, p, out, 0)
    put_rest(put, core, 1 - core, rp, out, 0)
    for copy in copies:
        copy.start()
    for copy in copies:
        copy.wait()


def pack_in_kernel(p0, p1, p2, far_x, far_y, out, bias):
    total = jnp.zeros((2, BLOCK), f32)
    for j in range(4):
        refs = {"first": p0, "x0": p1, "y0": p2, "x1": far_x, "y1": far_y}
        part, row = find(refs, 0, j, 512)
        out[j * 384 : (j + 1) * 384, :] = part[row : row + 384, :]
        part, row = find(refs, 0, j, 1536)
        for side in range(2):
            vectors = part[row + side * 16 : row + side * 16 + 16, :].astype(f32)
            total = total + vectors[6:8, :]
    bias[...] = total


def pack_out_kernel(turns, names, *refs):
    blocks, (out, sems) = dict(zip(names, refs)), refs[len(names) :]
    copies = []
    for n, k in enumerate(turns):
        for j in range(4):
            ref, row_in = find_ahead(blocks, k, j, 0)
            i = n * 4 + j
            copies.append(
                pltpu.make_async_copy(
                    ref.at[pl.ds(row_in, HALF)], out.at[pl.ds(i * HALF, HALF)], sems.at[i]
                )
            )
    for copy in copies:
        copy.start()
    for copy in copies:
        copy.wait()


def vectors_kernel(ids, *refs):
    blocks = dict(zip(MIDDLE, refs))
    six, inner, held, sems = refs[len(MIDDLE) :]
    copies = []
    for k in range(4):
        for j in range(4):
            ref, row_in = find_ahead(blocks, k, j, HALF)
            i = k * 4 + j
            copies.append(
                pltpu.make_async_copy(
                    ref.at[pl.ds(row_in, 32)], held.at[pl.ds(i * 32, 32)], sems.at[i]
                )
            )
    for copy in copies:
        copy.start()
    inner[...] = jnp.zeros(inner.shape, f32)
    for copy in copies:
        copy.wait()
    for j in range(4):
        chip = ids[0] ^ j
        for side in range(2):
            total = jnp.zeros((8, HALF), f32)
            for k in range(4):
                row = (k * 4 + j) * 32 + side * 16
                piece = held[row : row + 16, :HALF].astype(f32)
                total = total + piece[:8, :]
                at = ((ids[2] - k + QUARTERS) & (QUARTERS - 1)) * 2 + (chip >> 1)
                lane = pl.ds(pl.multiple_of((chip & 1) * BLOCK + side * HALF, HALF), HALF)
                here = lax.broadcasted_iota(jnp.int32, (8, HALF), 0) == at
                inner[:, lane] += jnp.where(here, piece[8:9, :], 0.0)
            lane = pl.multiple_of(chip * BLOCK + side * HALF, HALF)
            six[:, pl.ds(lane, HALF)] = total


def one_hot(ids, docs):
    down = segments(ids, docs, (LENGTH, 1), 0)
    lane = lax.broadcasted_iota(jnp.int32, (LENGTH, HEAD_DIM), 1)
    same = (lane == down).astype(bf16)
    other = jnp.where((lane < 8) & (lane != down), -1e30, 0.0).astype(bf16)
    return same, other


def attend_kernel(
    ids, docs, t0, t1, t2, t3, own, other, bias, q, k, v, w, m0, m1, m2, m3, lse, qs, ks, vs, mixed
):
    core = ids[1]
    for j in range(4):
        base = (ids[0] ^ j) * BLOCK
        for source, side in ((own, core), (other, 1 - core)):
            rows = pl.ds(pl.multiple_of(base + side * HALF, HALF), HALF)
            for i in range(3):
                at = (j * 3 + i) * HALF
                w[rows, i * BLOCK : (i + 1) * BLOCK] = source[at : at + HALF, :]
    for b, t in enumerate((t0, t1, t2, t3)):
        rows = slice(b * BLOCK, (b + 1) * BLOCK)
        made = None
        for j in range(4):
            at = t.shape[0] - LENGTH + j * BLOCK
            part = dot(t[at : at + BLOCK, :], w[j * BLOCK : (j + 1) * BLOCK, :])
            made = part if made is None else made + part
        q[rows, :] = (made[:, :BLOCK] + bias[0:1, :]).astype(bf16)
        k[rows, :] = made[:, BLOCK : 2 * BLOCK].astype(bf16)
        v[rows, :] = (made[:, 2 * BLOCK :] + bias[1:2, :]).astype(bf16)
    same, apart = one_hot(ids, docs)
    for h in range(4):
        cols = slice(h * HEAD_DIM, (h + 1) * HEAD_DIM)
        qs[h, :, :HEAD_DIM] = q[:, cols] * bf16(0.125)
        qs[h, :, HEAD_DIM:] = same
        ks[h, :, :HEAD_DIM] = k[:, cols]
        ks[h, :, HEAD_DIM:] = apart
        vs[h, :, :HEAD_DIM] = v[:, cols]
        vs[h, :, HEAD_DIM:] = jnp.zeros((LENGTH, HEAD_DIM), bf16)

    def one_block(b, carry):
        rows = pl.ds(pl.multiple_of(b * BLOCK, BLOCK), BLOCK)

        def scores_of(h):
            return dot(qs[h, rows, :], ks[h], NT)

        scores = scores_of(0)
        for h in range(4):
            later = scores_of(h + 1) if h < 3 else None
            cols = slice(h * HEAD_DIM, (h + 1) * HEAD_DIM)
            top = jnp.max(scores, -1, keepdims=True)
            expo = jnp.exp(scores - top)
            total = jnp.sum(expo, -1, keepdims=True)
            made = dot(expo.astype(bf16), vs[h])[:, :HEAD_DIM] * (1.0 / total)
            mixed[rows, cols] = made.astype(bf16)
            lse[rows, h : h + 1] = top + jnp.log(total)
            scores = later
        return carry

    lax.fori_loop(0, 4, one_block, 0)
    for b, m in enumerate((m0, m1, m2, m3)):
        m[...] = mixed[b * BLOCK : (b + 1) * BLOCK, :]


def project_kernel(ids, tokens, x0, x1, x2, x3, other_a, other_b, vectors, *refs):
    blocks = dict(zip(MIDDLE, refs))
    wo, normed, scale, low, sems = refs[len(MIDDLE) :]
    core = ids[1]
    copies = []
    for n, k in enumerate((0, 3, 1, 2)):
        for j in range(4):
            ref, row_in = find_ahead(blocks, k, j, 0)
            got, at = (other_a, n * 4 + j) if n < 3 else (other_b, j)
            for i, (source, start, side) in enumerate(
                ((ref, row_in, core), (got, at * HALF, 1 - core))
            ):
                rows = pl.ds(pl.multiple_of(k * BLOCK + side * HALF, HALF), HALF)
                copies.append(
                    pltpu.make_async_copy(
                        source.at[pl.ds(start, HALF)],
                        wo.at[rows, lanes(ids, j)],
                        sems.at[(n * 4 + j) * 2 + i],
                    )
                )
    for copy in copies:
        copy.start()
    total = tokens[...].astype(f32) + vectors[0:1, :]
    for copy in copies:
        copy.wait()
    for k, x in enumerate((x0, x1, x2, x3)):
        total = total + dot(x[...], wo[k * BLOCK : (k + 1) * BLOCK, :])
    centered = total - jnp.mean(total, -1, keepdims=True)
    r = lax.rsqrt(jnp.mean(centered * centered, -1, keepdims=True) + 1e-05)
    n = centered * r
    normed[...] = n
    scale[...] = jnp.broadcast_to(r, scale.shape)
    low[...] = (n * vectors[2:3, :] + vectors[3:4, :]).astype(bf16)


def w1_of(blocks, k, j, half):
    ref, row = find(blocks, k, j, half * BLOCK)
    return ref[row : row + BLOCK, :]


def w2_of(blocks, k, j):
    ref, row = find(blocks, k, j, SPLIT[k])
    return ref[row : row + 512, :]


def part_of(rows, j):
    return rows[:, j * BLOCK : (j + 1) * BLOCK]


def arrange(ids, rows, mine, theirs):
    for j in range(4):
        rows[:BLOCK, j * BLOCK : (j + 1) * BLOCK] = mine[:, lanes(ids, j)]
        rows[BLOCK:, j * BLOCK : (j + 1) * BLOCK] = theirs[:, lanes(ids, j)]


def gelu_parts(inner):
    density = jnp.exp2(inner * inner * -0.7213475204444817) * 0.3989422804014327
    base = 1.0 + 0.2316419 * jnp.abs(inner)
    t = pl.reciprocal(base, approx=True)
    t = t * (2.0 - base * t)
    tail = 1.330274429 * t - 1.821255978
    tail = tail * t + 1.781477937
    tail = tail * t - 0.356563782
    tail = (tail * t + 0.319381530) * t * density
    phi = jnp.where(inner >= 0.0, 1.0 - tail, tail)
    return inner * phi, phi + inner * density


def forward_kernel(turns, ids, mine, theirs, bias, *refs):
    names = WEIGHTS if turns[0] == 0 else LAST
    blocks, refs = dict(zip(names, refs)), refs[len(names) :]
    if turns[0] == 0:
        start = None
    else:
        start, refs = refs[:2], refs[2:]
    active, slope, out_mine, out_theirs, rows, total = refs
    arrange(ids, rows, mine, theirs)
    if start is not None:
        arrange(ids, total, *start)

    def inner_of(n, half):
        k = turns[n]
        at = ((ids[2] - k + QUARTERS) & (QUARTERS - 1)) * 2 + ids[1]
        offset = bias[pl.ds(at, 1), half * BLOCK : (half + 1) * BLOCK]
        total = dot(part_of(rows, 0), w1_of(blocks, k, 0, half)) + offset
        for j in range(1, 4):
            total = total + dot(part_of(rows, j), w1_of(blocks, k, j, half))
        return total

    steps = [(n, half) for n in range(len(turns)) for half in range(2)]
    inner = inner_of(*steps[0])
    for i, (n, half) in enumerate(steps):
        later = inner_of(*steps[i + 1]) if i + 1 < len(steps) else None
        span = slice(half * BLOCK, (half + 1) * BLOCK)
        deep = slice(n * 512, (n + 1) * 512)
        made, grown = gelu_parts(inner)
        active[deep, span] = made.astype(bf16)
        slope[deep, span] = grown.astype(bf16)
        if half == 1:
            for j in range(4):
                part = dot(active[deep, :], w2_of(blocks, turns[n], j))
                if n == 0 and start is None:
                    total[:, j * BLOCK : (j + 1) * BLOCK] = part
                else:
                    total[:, j * BLOCK : (j + 1) * BLOCK] += part
        inner = later
    for j in range(4):
        span = slice(j * BLOCK, (j + 1) * BLOCK)
        out_mine[:, lanes(ids, j)] = total[:BLOCK, span]
        out_theirs[:, lanes(ids, j)] = total[BLOCK:, span]


def second_kernel(normed, mine, got, vectors, cot, out, grad, low, sums):
    gain, shift = vectors[4:5, :], vectors[5:6, :]
    total = normed[...] * vectors[2:3, :] + vectors[3:4, :] + (mine[...] + got[...])
    total = total + vectors[1:2, :]
    centered = total - jnp.mean(total, -1, keepdims=True)
    r = lax.rsqrt(jnp.mean(centered * centered, -1, keepdims=True) + 1e-05)
    n = centered * r
    out[...] = (n * gain + shift).astype(bf16)
    up = cot[...].astype(f32)
    back = norm_back(up, n, r, gain)
    grad[...] = back
    low[...] = back.astype(bf16)
    sums[0:1, :] = jnp.sum(back, 0, keepdims=True)
    sums[1:2, :] = jnp.sum(up * n, 0, keepdims=True)
    sums[2:3, :] = jnp.sum(up, 0, keepdims=True)


def backward_kernel(ids, mine, theirs, slope0, slope1, *refs):
    blocks = dict(zip(ALL, refs))
    back, out_mine, out_theirs, sums, rows = refs[len(ALL) :]
    arrange(ids, rows, mine, theirs)
    sums[...] = jnp.zeros(sums.shape, f32)
    for k in range(4):
        span = slice(k * 512, (k + 1) * 512)
        made = dot(part_of(rows, 0), w2_of(blocks, k, 0), NT)
        for j in range(1, 4):
            made = made + dot(part_of(rows, j), w2_of(blocks, k, j), NT)
        grown = slope0[span, :] if k < 3 else slope1[...]
        made = (made * grown.astype(f32)).astype(bf16)
        back[span, :] = made
        at = ((ids[2] - k + QUARTERS) & (QUARTERS - 1)) * 2 + ids[1]
        sums[pl.ds(at, 1), :] = jnp.sum(made.astype(f32), 0, keepdims=True)
    for j in range(4):
        for n, out in enumerate((out_mine, out_theirs)):
            total = None
            for k in range(4):
                rows_at = k * 512 + n * BLOCK
                for half in range(2):
                    cols = slice(half * BLOCK, (half + 1) * BLOCK)
                    part = dot(back[rows_at : rows_at + BLOCK, cols], w1_of(blocks, k, j, half), NT)
                    total = part if total is None else total + part
            out[:, lanes(ids, j)] = total.astype(out.dtype)


def weights_kernel(ids, active1, back1, active2, back2, mine, theirs, gmine, gtheirs, *outs):
    for j in range(4):
        at = lanes(ids, j)
        for active, back, out in ((active1, back1, outs[j]), (active2, back2, outs[4 + j])):
            left = dot(mine[:, at], back[:BLOCK, :], TN) + dot(theirs[:, at], back[BLOCK:, :], TN)
            out[:BLOCK, :] = left[:, :BLOCK].astype(bf16)
            out[BLOCK:512, :] = left[:, BLOCK:].astype(bf16)
            out[512:1024, :] = (
                dot(active[:BLOCK, :], gmine[:, at], TN)
                + dot(active[BLOCK:, :], gtheirs[:, at], TN)
            ).astype(bf16)


def first_kernel(second, mine, got, normed, scale, vectors, wo, grad, low, g0, g1, g2, g3, sums):
    hidden = second[...] + mine[...] + got[...].astype(f32)
    n = normed[...]
    back = norm_back(hidden, n, scale[:, :1], vectors[2:3, :])
    grad[...] = back
    rounded = back.astype(bf16)
    low[...] = rounded
    for k, g in enumerate((g0, g1, g2, g3)):
        g[...] = dot(rounded, wo[k * BLOCK : (k + 1) * BLOCK, :], NT).astype(bf16)
    sums[0:1, :] = jnp.sum(back, 0, keepdims=True)
    sums[1:2, :] = jnp.sum(hidden * n, 0, keepdims=True)
    sums[2:3, :] = jnp.sum(hidden, 0, keepdims=True)


def output_grad_kernel(ids, x0, x1, x2, x3, low, first, second, inner, own, send, made):
    core = ids[1]
    sums = jnp.concatenate([first[...], second[...], jnp.zeros((2, first.shape[1]), f32)], 0)
    for k, x in enumerate((x0, x1, x2, x3)):
        made[...] = dot(x[...], low[...], TN)
        for out, side in ((own, core), (send, 1 - core)):
            rows = pl.ds(pl.multiple_of(side * HALF, HALF), HALF)
            for j in range(4):
                at = j * 576 + k * 144
                out[at : at + HALF, :] = made[rows, lanes(ids, j)].astype(bf16)
    made[0:8, :] = sums
    for j in range(4):
        chip = ids[0] ^ j
        there = ((chip >> 1) == core).astype(f32)
        for k in range(4):
            at = ((ids[2] - k + QUARTERS) & (QUARTERS - 1)) * 2 + core
            row = inner[pl.ds(at, 1), :]
            row = jnp.where((chip & 1) == 0, row[:, :BLOCK], row[:, BLOCK:]) * there
            six = made[0:8, lanes(ids, j)]
            here = lax.broadcasted_iota(jnp.int32, (8, BLOCK), 0) == 6
            piece = jnp.concatenate([jnp.where(here, row, six), jnp.zeros((8, BLOCK), f32)], 0)
            at = j * 576 + k * 144 + HALF
            own[at : at + 16, :] = piece.astype(bf16)
            send[at : at + 16, :] = jnp.zeros((16, BLOCK), bf16)


def attend_back_kernel(
    heads, ids, docs, q, k, v, lse, m0, m1, m2, m3, g0, g1, g2, g3, out, sums, *scratch
):
    qs, ks, vs, gs, kt, ktot, vtot, qtot, stats = scratch
    count = len(heads)
    same, apart = one_hot(ids, docs)
    nothing = jnp.zeros((LENGTH, HEAD_DIM), bf16)
    centres = []
    for i, h in enumerate(heads):
        cols = slice(h * HEAD_DIM, (h + 1) * HEAD_DIM)
        qs[i, :, :HEAD_DIM] = q[:, cols] * bf16(0.125)
        qs[i, :, HEAD_DIM:] = same
        ks[i, :, :HEAD_DIM] = k[:, cols]
        ks[i, :, HEAD_DIM:] = apart
        vs[i, :, :HEAD_DIM] = v[:, cols]
        vs[i, :, HEAD_DIM:] = nothing
        gs[i, :, HEAD_DIM:] = nothing
        parts = []
        for b, (g, mixed) in enumerate(((g0, m0), (g1, m1), (g2, m2), (g3, m3))):
            gs[i, b * BLOCK : (b + 1) * BLOCK, :HEAD_DIM] = g[:, cols]
            product = g[:, cols].astype(f32) * mixed[:, cols].astype(f32)
            parts.append(jnp.sum(product, -1, keepdims=True))
        centres.append(jnp.concatenate(parts, 0))
        kt[i] = jnp.transpose(ks[i])
    centres.append(jnp.zeros((LENGTH, HALF - count), f32))
    stats[0] = jnp.transpose(jnp.concatenate(centres, 1))
    stats[1] = jnp.transpose(lse[...])
    vtot[...] = jnp.zeros(vtot.shape, f32)
    ktot[...] = jnp.zeros(ktot.shape, f32)

    def one_block(b, carry):
        rows = pl.ds(pl.multiple_of(b * BLOCK, BLOCK), BLOCK)

        def pair(i):
            return dot(ks[i], qs[i, rows, :], NT), dot(vs[i], gs[i, rows, :], NT)

        scores, dots = pair(0)
        for i in range(count):
            later = pair(i + 1) if i + 1 < count else (None, None)
            shares = jnp.exp(scores - stats[1, heads[i] : heads[i] + 1, rows])
            back = (shares * (dots - stats[0, i : i + 1, rows])).astype(bf16)
            vtot[i] += dot(shares.astype(bf16), gs[i, rows, :])
            ktot[i] += dot(back, qs[i, rows, :])
            qtot[i, :, rows] = dot(kt[i], back)
            scores, dots = later
        return carry

    lax.fori_loop(0, 4, one_block, 0)
    size = count * HEAD_DIM
    for i in range(count):
        made = (jnp.transpose(qtot[i])[:, :HEAD_DIM] * 0.125, ktot[i], vtot[i])
        for n, value in enumerate(made):
            at = n * size + i * HEAD_DIM
            out[:, at : at + HEAD_DIM] = value[:, :HEAD_DIM].astype(bf16)
    sums[0:1, :] = jnp.sum(out[:, :size].astype(f32), 0, keepdims=True)
    sums[1:2, :] = jnp.sum(out[:, 2 * size :].astype(f32), 0, keepdims=True)


def token_grad_kernel(low, high, w, wo, d0, d1, d2, d3, dqkv):
    for part, at in ((low, 0), (high, HALF)):
        for i in range(3):
            dqkv[:, i * BLOCK + at : i * BLOCK + at + HALF] = part[:, i * HALF : (i + 1) * HALF]
    for b, out in ((1, d1), (2, d2), (3, d3), (0, d0)):
        rows = slice(b * BLOCK, (b + 1) * BLOCK)
        out[:BLOCK, :] = dot(dqkv[rows, :], w[...], NT).astype(bf16)
        for i in range(3):
            at = b * 144 + i * 48
            out[BLOCK:, i * BLOCK : (i + 1) * BLOCK] = wo[at : at + 48, :]
        out[BLOCK:, 3 * BLOCK :] = jnp.zeros((48, BLOCK), bf16)


def input_grad_kernel(ids, t0, t1, t2, t3, dqkv, sums, own, send, made):
    core = ids[1]
    vectors = jnp.concatenate([sums[...], jnp.zeros((14, BLOCK), f32)], 0).astype(bf16)
    for j in range(4):
        for out in (own, send):
            out[j * 400 + 384 : (j + 1) * 400, :] = vectors
    for j in range(4):
        total = None
        for b, t in enumerate((t0, t1, t2, t3)):
            at = pl.multiple_of(t.shape[0] - LENGTH + (ids[0] ^ j) * BLOCK, 32)
            part = dot(t[pl.ds(at, BLOCK), :], dqkv[b * BLOCK : (b + 1) * BLOCK, :], TN)
            total = part if total is None else total + part
        made[...] = total
        for out, side in ((own, core), (send, 1 - core)):
            rows = pl.ds(pl.multiple_of(side * HALF, HALF), HALF)
            for i in range(3):
                to = j * 400 + i * HALF
                out[to : to + HALF, :] = made[rows, i * BLOCK : (i + 1) * BLOCK].astype(bf16)


def body_for(dp, tensor):
    fast = dp == 8 and tensor == 4
    ring_pairs = [(i, (i + 1) % tensor) for i in range(tensor)]

    def flip(value, bit, axis="dp", size=dp):
        return lax.ppermute(value, axis, [(i, i ^ bit) for i in range(size)])

    def ring(value):
        return lax.ppermute(value, "tensor", ring_pairs)

    def swap(value):
        return flip(value, 1)

    def sum_all(value, over_tensor=True):
        bit = dp >> 1
        while bit:
            value = value + flip(value, bit)
            bit >>= 1
        bit = 1
        while over_tensor and bit < tensor:
            value = value + flip(value, bit, "tensor", tensor)
            bit <<= 1
        return value

    def in_order(core, own, got, axis):
        return jnp.where(
            core == 0,
            jnp.concatenate([own, got], axis),
            jnp.concatenate([got, own], axis),
        )

    def after(value, *others):
        return lax.optimization_barrier((value, *others))[0]

    def assemble(ids, tokens, prepared, wq, wk, wv, w1, w2):
        pairs = [
            ((p * tensor + i), ((p ^ 1) * tensor + (i + tensor - 1) % tensor))
            for p in range(dp)
            for i in range(tensor)
        ]
        back = [(i, (i + tensor - 1) % tensor) for i in range(tensor)]
        made = call(
            assemble_kernel,
            "assemble",
            (ids, w1, swap(w1), w2, swap(w2), prepared, swap(prepared), wq, wk, wv, tokens),
            [SMEM] + [HBM] * 10,
            [shape((1568, BLOCK), bf16), shape((2208, BLOCK), bf16)],
            scratch=[pltpu.SemaphoreType.DMA((31,))],
        )
        gated = after(prepared, made[0])
        ahead = call(
            ahead_kernel,
            "ahead",
            (ids, lax.ppermute(gated, "tensor", back), lax.ppermute(gated, ("dp", "tensor"), pairs)),
            [SMEM] + [HBM] * 2,
            [shape((HALF + 32, BLOCK), bf16)],
            scratch=[pltpu.SemaphoreType.DMA((6,))],
        )[0]
        return made, ahead

    def gather_any(core, z, wq, wk, wv, wo, w1, w2):
        def whole(value, dim):
            value = lax.all_gather(value, "dp", axis=dim, tiled=True)
            return value

        def quarters(value):
            value = lax.all_gather(value, "tensor", axis=0, tiled=False)
            return jnp.take(value, (z - jnp.arange(tensor)) % tensor, axis=0)

        a = quarters(lax.dynamic_slice_in_dim(whole(w1, 0), core * 512, 512, 1))
        b = quarters(lax.dynamic_slice_in_dim(whole(w2, 1), core * 512, 512, 0))
        c = quarters(lax.dynamic_slice_in_dim(whole(wo, 1), core * HALF, HALF, 0))
        qkv = jnp.stack([whole(wq, 0), whole(wk, 0), whole(wv, 0)])
        qkv = qkv.reshape(3, 4, 2, HALF, BLOCK).transpose(2, 1, 0, 3, 4).reshape(2, 1536, BLOCK)
        blocks, parts = {}, {}
        for k in range(4):
            for j in range(4):
                span = slice(j * BLOCK, (j + 1) * BLOCK)
                left = [a[k, span, :BLOCK], a[k, span, BLOCK:]]
                if k == 0:
                    left.append(jnp.zeros((384, BLOCK), bf16))
                right = [b[k][:, span], c[k][:, span], jnp.zeros((32, BLOCK), bf16)]
                if j < 3:
                    parts[PLACES[k][j]] = left + right
                else:
                    parts[PLACES[k][3]], parts[PLACES[k][4]] = left, right
        for j in range(4):
            piece = c[3][:, j * BLOCK : (j + 1) * BLOCK]
            parts[AHEAD[j]] = [piece, jnp.zeros((32, BLOCK), bf16)]
        for name in ALL + ("ahead",):
            made = [parts[place] for place in sorted(p for p in parts if p[0] == name)]
            blocks[name] = jnp.concatenate(sum(made, []), 0)
        return blocks, qkv[core], qkv[1 - core]

    def body(
        tokens,
        cotangent,
        doc_lengths,
        query_weight,
        key_weight,
        value_weight,
        output_weight,
        inner_weight,
        outer_weight,
        query_offset,
        value_offset,
        inner_offset,
        output_offset,
        outer_offset,
        first_gain,
        first_shift,
        second_gain,
        second_shift,
    ):
        place = lax.axis_index("dp")
        z = lax.axis_index("tensor")
        core = place & 1
        chip = (place >> 1) if fast else jnp.zeros_like(place)
        ids = jnp.stack([chip, core, z, place]).astype(jnp.int32)
        rows = tokens.shape[0]
        width = tokens.shape[1]

        six = jnp.stack(
            [output_offset, outer_offset, first_gain, first_shift, second_gain, second_shift]
        )
        two = jnp.stack([query_offset, value_offset])
        weights = (query_weight, key_weight, value_weight)
        t = [tokens]
        if fast:
            prepared = call(
                prepare_kernel,
                "prepare",
                (ids, six, two, inner_offset[None], output_weight),
                [SMEM] + [VMEM] * 4,
                [shape((BLOCK + 32, HALF), bf16)],
            )[0]
            (first, block), ahead = assemble(
                ids, tokens, prepared, *weights, inner_weight, outer_weight
            )

            def join(*outs):
                inputs = []
                for _, source, _, _ in sum(outs, []):
                    if not any(source is other for other in inputs):
                        inputs.append(source)

                def index(source):
                    return [other is source for other in inputs].index(True)

                spans = [[(index(a), row, size) for _, a, row, size in out] for out in outs]
                return call(
                    functools.partial(join_kernel, spans),
                    "join",
                    tuple(inputs),
                    [VMEM] * len(inputs),
                    [shape((sum(size for _, _, size in span), BLOCK), bf16) for span in spans],
                )

            x0, y0, z1 = flip(first, 2), flip(first, 4), ring(block)
            xm, ym = join(
                [(0, z1, 0, 1184), (0, y0, 896, 672), (0, ahead, 0, 160)],
                [(0, z1, 0, 1184), (0, x0, 0, 896), (0, ahead, 0, 160)],
            )
            x1, y1, z2 = flip(xm, 2), flip(ym, 4), ring(after(z1, xm))
            xm, ym, tokens2, part2 = join(
                [(0, z2, 0, 1184), (0, y1, 512, 672)],
                [(0, z2, 0, 1184), (0, x1, 0, 512), (0, x1, 1856, 160)],
                [(0, z2, 1184, 1024)],
                [(0, z2, 0, 1184)],
            )
            x2, y2, t3, z3 = flip(xm, 2), flip(ym, 4), ring(tokens2), ring(part2)
            t = [block, z1, z2, t3]
            own_in, qv_bias = call(
                pack_in_kernel,
                "pack_in",
                (first, x0, y0, x1, y1),
                [VMEM] * 5,
                [shape((1536, BLOCK), bf16), shape((2, BLOCK), f32)],
            )
            other_in = swap(own_in)
        else:
            piece = six.shape[1]
            field = jnp.arange(width) // piece == place * tensor + z
            six = jnp.where(field, jnp.tile(six.astype(f32), (1, width // piece)), 0)
            piece = two.shape[1]
            field = jnp.arange(width) // piece == z * dp + place
            two = jnp.where(field, jnp.tile(two.astype(f32), (1, width // piece)), 0)
            piece = inner_offset.shape[0]
            wide = piece * dp * tensor
            field = jnp.arange(wide) // piece == z * dp + place
            one = jnp.where(field, jnp.tile(inner_offset.astype(f32), wide // piece), 0)
            vectors = sum_all(jnp.concatenate([six, two, one.reshape(4, width)], 0))
            qv_bias = lax.dynamic_slice(vectors, (6, z * BLOCK), (2, BLOCK))
            inner_bias = vectors[8:12].reshape(8, 512)
            vectors = vectors[:8]
            blocks, own_in, other_in = gather_any(
                core, z, *weights, output_weight, inner_weight, outer_weight
            )
            for _ in range(3):
                t.append(ring(t[-1]))
            t = [
                jnp.concatenate([p[:, j * BLOCK : (j + 1) * BLOCK] for j in range(4)], 0)
                for p in t
            ]

        square = shape((LENGTH, BLOCK), bf16)
        tile = shape((BLOCK, BLOCK), bf16)
        q, k, v, w_in, m0, m1, m2, m3, lse = call(
            attend_kernel,
            "attend",
            (ids, doc_lengths, *t, own_in, other_in, qv_bias),
            [SMEM, SMEM] + [VMEM] * 7,
            [square] * 3
            + [shape((width, 3 * BLOCK), bf16)]
            + [tile] * 4
            + [shape((LENGTH, HALF), f32)],
            scratch=[pltpu.VMEM((4, LENGTH, HALF), bf16)] * 3 + [pltpu.VMEM((LENGTH, BLOCK), bf16)],
        )

        def shift(value, by):
            return lax.ppermute(value, "tensor", [(i, (i - by) % tensor) for i in range(tensor)])

        if fast:
            z3, x2, y2, m0 = lax.optimization_barrier((z3, x2, y2, m0))
            xm, ym = join(
                [(0, z3, 0, 1184), (0, y2, 512, 672)],
                [(0, z3, 0, 1184), (0, x2, 0, 512)],
            )
            x3, y3 = flip(xm, 2), flip(ym, 4)
        x = [m0, shift(m3, 3), shift(m2, 2), shift(m1, 1)]

        def pack_out(turns, names):
            size = len(turns) * 4
            return swap(
                call(
                    functools.partial(pack_out_kernel, turns, names),
                    "pack_out",
                    tuple(blocks[name] for name in names),
                    [HBM] * len(names),
                    [shape((size * HALF, BLOCK), bf16)],
                    scratch=[pltpu.SemaphoreType.DMA((size,))],
                )[0]
            )

        if fast:
            blocks = {
                "first": first,
                "x0": x0,
                "y0": y0,
                "z1": z1,
                "x1": x1,
                "y1": y1,
                "z2": z2,
                "x2": x2,
                "y2": y2,
                "ahead": ahead,
            }
        other_a = pack_out((0, 3, 1), EARLY)
        if fast:
            x3, y3, *x = lax.optimization_barrier((x3, y3, *x))
            xm, ym = join([(0, y3, 512, 672)], [(0, x3, 0, 512)])
            blocks.update(z3=z3, x3=x3, y3=y3, x4=flip(xm, 2), y4=flip(ym, 4))
            vectors, inner_bias = call(
                vectors_kernel,
                "vectors",
                (ids, *[blocks[name] for name in MIDDLE]),
                [SMEM] + [HBM] * len(MIDDLE),
                [shape((8, width), f32), shape((8, 512), f32)],
                scratch=[pltpu.VMEM((512, BLOCK), bf16), pltpu.SemaphoreType.DMA((16,))],
            )
        other_b = pack_out((2,), MIDDLE)
        wide_f = shape((rows, width), f32)
        wide_b = shape((rows, width), bf16)
        w_out, normed1, scale1, hidden_low = call(
            project_kernel,
            "project",
            (ids, tokens, *x, other_a, other_b, vectors, *[blocks[name] for name in MIDDLE]),
            [SMEM] + [VMEM] * 5 + [HBM] * 2 + [VMEM] + [HBM] * len(MIDDLE),
            [shape((width, width), bf16), wide_f, shape((rows, HALF), f32), wide_b],
            scratch=[pltpu.SemaphoreType.DMA((32,))],
        )
        hidden_other = swap(hidden_low)

        def forward(turns, *start):
            tall = shape((len(turns) * 512, 512), bf16)
            names = WEIGHTS if turns[0] == 0 else LAST
            return call(
                functools.partial(forward_kernel, turns),
                "forward",
                (ids, hidden_low, hidden_other, inner_bias)
                + tuple(blocks[name] for name in names)
                + start,
                [SMEM] + [VMEM] * (3 + len(names) + len(start)),
                [tall, tall, wide_f, wide_f],
                scratch=[
                    pltpu.VMEM((2 * rows, width), bf16),
                    pltpu.VMEM((2 * rows, width), f32),
                ],
            )

        active0, slope0, out_own, out_send = forward((0, 1, 2))
        active1, slope1, out_own, out_send = forward((3,), out_own, out_send)
        result, second_grad, second_low, second_sums = call(
            second_kernel,
            "second",
            (
                normed1,
                out_own,
                swap(out_send),
                vectors,
                cotangent,
            ),
            [VMEM] * 5,
            [wide_b, wide_f, wide_b, shape((3, width), f32)],
        )
        second_other = swap(second_low)
        tall = shape((2048, 512), bf16)
        back, grad_own, grad_send, inner_sums = call(
            backward_kernel,
            "backward",
            (ids, second_low, second_other, slope0, slope1, *[blocks[name] for name in ALL]),
            [SMEM] + [VMEM] * (4 + len(ALL)),
            [tall, wide_f, wide_b, shape((8, 512), f32)],
            scratch=[pltpu.VMEM((2 * rows, width), bf16)],
        )

        def weights_of(turns, *others):
            def at(turn):
                return pl.BlockSpec((512, 512), lambda i: (turn, 0))

            def active_of(turn):
                return (active0, at(turn)) if turn < 3 else (active1, at(0))

            (a, a_at), (b, b_at) = active_of(turns[0]), active_of(turns[1])
            made = call(
                weights_kernel,
                "weights",
                (
                    ids,
                    a,
                    back,
                    b,
                    back,
                    hidden_low,
                    hidden_other,
                    second_low,
                    after(second_other, *others),
                ),
                [SMEM, a_at, at(turns[0]), b_at, at(turns[1])] + [VMEM] * 4,
                [shape((1024, BLOCK), bf16)] * 8,
                grid=(1,),
            )
            return {turns[0]: made[:4], turns[1]: made[4:]}

        grad_got = swap(grad_send)
        grads = weights_of((1, 2))
        first_grad, first_low, g0, g1, g2, g3, first_sums = call(
            first_kernel,
            "first",
            (
                second_grad,
                grad_own,
                after(grad_got, *grads[1]),
                normed1,
                scale1,
                vectors,
                w_out,
            ),
            [VMEM] * 7,
            [wide_f, wide_b] + [tile] * 4 + [shape((3, width), f32)],
        )
        g = [g0, shift(g3, 3), shift(g2, 2), shift(g1, 1)]
        grads.update(weights_of((3, 0), first_low))

        def meet(parts, turn):
            own, by_x, by_y, far = parts
            if turn % 2 == 0:
                return [own, by_x + flip(far, 4), by_y]
            return [own, by_x, by_y + flip(far, 2)]

        out_part = shape((2304, BLOCK), bf16)
        wo_own, wo_send = call(
            output_grad_kernel,
            "output_grad",
            (ids, *x, first_low, first_sums, second_sums, inner_sums),
            [SMEM] + [VMEM] * 8,
            [out_part, out_part],
            scratch=[pltpu.VMEM((BLOCK, width), f32)],
        )
        if fast:
            gated = lax.optimization_barrier(
                (grads[1][2], grads[2][1], grads[3][3], grads[0][3], *g[1:])
            )
            grads[1], grads[2] = list(grads[1]), list(grads[2])
            grads[3], grads[0] = list(grads[3]), list(grads[0])
            grads[1][2], grads[2][1] = gated[:2]
            met = {turn: meet(grads[turn], turn) for turn in (1, 2)}
            wo_got = swap(wo_send)

            def send(turn):
                return flip(met[turn][1], 2), flip(met[turn][2], 4)

            sent = {1: send(1)}

            def settle(turn, moving=None):
                total = (
                    met[turn][0].astype(f32)
                    + sent[turn][0].astype(f32)
                    + sent[turn][1].astype(f32)
                )
                return total if moving is None else total + moving.astype(f32)

        def attend_back(heads, g):
            size = len(heads) * HEAD_DIM
            return call(
                functools.partial(attend_back_kernel, heads),
                "attend_back",
                (ids, doc_lengths, q, k, v, lse, m0, m1, m2, m3, *g),
                [SMEM, SMEM] + [VMEM] * 12,
                [shape((LENGTH, 3 * size), bf16), shape((2, size), f32)],
                scratch=[pltpu.VMEM((len(heads), LENGTH, HALF), bf16)] * 4
                + [pltpu.VMEM((len(heads), HALF, LENGTH), bf16)]
                + [pltpu.VMEM((len(heads), LENGTH, HALF), f32)] * 2
                + [pltpu.VMEM((len(heads), HALF, LENGTH), f32)]
                + [pltpu.VMEM((2, HALF, LENGTH), f32)],
            )

        if fast:
            wo_total = (wo_own.astype(f32) + wo_got.astype(f32)).astype(bf16)
            wo_parts = [wo_total[j * 576 : (j + 1) * 576] for j in range(4)]
            wo_far = flip(wo_parts[3], 2)
            g[0] = after(g[0], met[1][2], met[2][1], wo_far)
        dqkv_low, sums_low = attend_back((0, 1), g)
        if fast:
            wo_x = flip(wo_parts[1], 2)
            wo_y = flip(wo_parts[2] + wo_far, 4)
            gated = (*sent[1], *met[2][1:3], grads[3][3], grads[0][3], dqkv_low)
            gated = lax.optimization_barrier(gated)
            sent[1] = gated[:2]
            met[2][1:3] = gated[2:4]
            grads[3][3], grads[0][3] = gated[4:6]
            sent[2] = send(2)
            total1 = settle(1).astype(bf16)
            moving1 = ring(total1)
            g[0] = after(g[0], dqkv_low, total1)
        dqkv_high, sums_high = attend_back((2, 3), g)
        head_sums = jnp.concatenate([sums_low, sums_high], 1)
        if fast:
            wo_total = wo_parts[0].astype(f32) + wo_x.astype(f32) + wo_y.astype(f32)
            wo_total = after(wo_total.astype(bf16), dqkv_high)
        else:
            wo_total = wo_own[:576]
        moved = shape((rows + 48, width), bf16)
        d0, d1, d2, d3, dqkv = call(
            token_grad_kernel,
            "token_grad",
            (dqkv_low, dqkv_high, w_in, wo_total),
            [VMEM] * 4,
            [moved] * 4 + [shape((LENGTH, 3 * BLOCK), bf16)],
        )
        if fast:
            gated = lax.optimization_barrier((*grads[3][1:3], *grads[0][1:3], d1))
            met[3] = meet([grads[3][0], *gated[0:2], grads[3][3]], 3)
            met[0] = meet([grads[0][0], *gated[2:4], grads[0][3]], 0)
            sent.update({turn: send(turn) for turn in (3, 0)})
            total2 = settle(2, moving1).astype(bf16)
            moving2 = ring(total2)
            dqkv = after(dqkv, met[3][2], met[0][1])
        in_part = shape((1600, BLOCK), bf16)
        in_own, in_send = call(
            input_grad_kernel,
            "input_grad",
            (ids, *t, dqkv, head_sums),
            [SMEM] + [VMEM] * 6,
            [in_part, in_part],
            scratch=[pltpu.VMEM((BLOCK, 3 * BLOCK), f32)],
        )

        def add(left, right):
            return (left.astype(f32) + right.astype(f32)).astype(bf16)

        moving = ring(d1)
        if fast:
            moving, in_send = lax.optimization_barrier((moving, in_send))
            moving = ring(add(moving, d2))
            total3 = settle(3, moving2).astype(bf16)
            moving3 = ring(total3)
            in_total = add(in_own, swap(in_send))
            in_parts = [in_total[j * 400 : (j + 1) * 400] for j in range(4)]
            in_far = flip(in_parts[3], 2)
            moving = ring(add(moving, d3))
            in_x = flip(in_parts[1], 2)
            in_y = flip(in_parts[2] + in_far, 4)
            mine = settle(0, moving3)
        else:
            moving = ring(add(moving, d2))
            moving = ring(add(moving, d3))
        moving = moving.astype(f32) + d0.astype(f32)
        tokens_grad = first_grad + moving[:rows]

        if fast:
            left = mine[:512].reshape(2, 2, HALF, BLOCK)
            right = mine[512:]

            def sides(side):
                a = lax.dynamic_index_in_dim(left, side, 1, False)
                b = lax.dynamic_slice_in_dim(right, side * HALF, HALF, 1)
                return a, b

            a, b = sides(1 - core)
            got = swap(
                jnp.concatenate(
                    [a[0, :, :HALF], a[0, :, HALF:], a[1, :, :HALF], a[1, :, HALF:], b], 0
                ).astype(bf16)
            ).astype(f32)
            a, b = sides(core)
            ga = jnp.concatenate([got[i * HALF : (i + 1) * HALF] for i in range(4)], 1)
            inner_grad = in_order(core, jnp.concatenate([a[0], a[1]], 1), ga, 1)
            outer_grad = in_order(core, b, got[512:], 0)

            total = jnp.concatenate(
                [moving[rows:, i * BLOCK : (i + 1) * BLOCK] for i in range(3)], 0
            )
            got = swap(lax.dynamic_slice_in_dim(total, (1 - core) * HALF, HALF, 1))
            total = lax.dynamic_slice_in_dim(total, core * HALF, HALF, 1)
            output_grad = in_order(core, total[:HALF], got[:HALF], 0)
            sums = total[HALF:] + got[HALF:]
            six = lax.dynamic_slice(sums, (0, z * 32), (6, 32))
            offset_inner = sums[6]

            total = in_parts[0].astype(f32) + in_x.astype(f32) + in_y.astype(f32)
            query_grad, key_grad, value_grad = [
                total[i * HALF : (i + 1) * HALF] for i in range(3)
            ]
            head_sums = total[384:386]
        else:
            def scatter(value, dim):
                return lax.psum_scatter(value, "dp", scatter_dimension=dim, tiled=True)

            def quarter(parts):
                found = jnp.stack(parts).astype(f32)
                found = jnp.take(found, (z - jnp.arange(tensor)) % tensor, axis=0)
                return lax.psum_scatter(found, "tensor", scatter_dimension=0, tiled=False)

            def half(value, dim):
                field = jnp.zeros_like(value)
                return jnp.where(
                    core == 0,
                    jnp.concatenate([value, field], dim),
                    jnp.concatenate([field, value], dim),
                )

            a = quarter(
                [
                    jnp.concatenate(
                        [jnp.concatenate([p[:BLOCK], p[BLOCK:512]], 1) for p in grads[turn]], 0
                    )
                    for turn in range(4)
                ]
            )
            b = quarter(
                [jnp.concatenate([p[512:1024] for p in grads[turn]], 1) for turn in range(4)]
            )
            inner_grad = scatter(half(a, 1), 0)
            outer_grad = scatter(half(b, 0), 1)

            def heads(value):
                value = value.reshape(4, 4, 144, BLOCK)[:, :, :HALF]
                return value.transpose(1, 2, 0, 3).reshape(4, HALF, width)

            mine, theirs = quarter(list(heads(wo_own))), quarter(list(heads(wo_send)))
            output_grad = scatter(in_order(core, mine, theirs, 0), 1)
            own, send = [
                p.astype(f32).reshape(4, 400, BLOCK)[:, :384].reshape(4, 3, HALF, BLOCK)
                for p in (in_own, in_send)
            ]
            both = jnp.where(core == 0, jnp.stack([own, send], 1), jnp.stack([send, own], 1))
            both = both.transpose(2, 0, 1, 3, 4).reshape(3, width, BLOCK)
            query_grad, key_grad, value_grad = [scatter(both[i], 0) for i in range(3)]

            sums = jnp.concatenate([first_sums, second_sums, inner_sums.reshape(4, width)], 0)
            sums = sum_all(sums)
            head_sums = sum_all(head_sums, False)
            piece = width // (dp * tensor)
            six = lax.dynamic_slice_in_dim(sums[:6], (place * tensor + z) * piece, piece, 1)
            piece = inner_offset.shape[0]
            offset_inner = lax.dynamic_slice_in_dim(
                sums[6:].reshape(-1), (z * dp + place) * piece, piece, 0
            )

        head_sums = lax.dynamic_slice_in_dim(head_sums, place * (BLOCK // dp), BLOCK // dp, 1)
        return (
            result,
            tokens_grad,
            query_grad,
            key_grad,
            value_grad,
            output_grad,
            inner_grad,
            outer_grad,
            head_sums[0],
            head_sums[1],
            offset_inner,
            six[0],
            six[3],
            six[1],
            six[2],
            six[4],
            six[5],
        )

    return body


def solution(mesh):
    return jax.shard_map(
        body_for(mesh.shape["dp"], mesh.shape["tensor"]),
        mesh=mesh,
        in_specs=(
            P(("dp", "tensor"), None),
            P(("dp", "tensor"), None),
            P("dp", None),
            P("dp", "tensor"),
            P("dp", "tensor"),
            P("dp", "tensor"),
            P("tensor", "dp"),
            P("dp", "tensor"),
            P("tensor", "dp"),
            P(("tensor", "dp")),
            P(("tensor", "dp")),
            P(("tensor", "dp")),
            P(("dp", "tensor")),
            P(("dp", "tensor")),
            P(("dp", "tensor")),
            P(("dp", "tensor")),
            P(("dp", "tensor")),
            P(("dp", "tensor")),
        ),
        out_specs=(
            P(("dp", "tensor"), None),
            P(("dp", "tensor"), None),
            P("dp", "tensor"),
            P("dp", "tensor"),
            P("dp", "tensor"),
            P("tensor", "dp"),
            P("dp", "tensor"),
            P("tensor", "dp"),
            P(("tensor", "dp")),
            P(("tensor", "dp")),
            P(("tensor", "dp")),
            P(("dp", "tensor")),
            P(("dp", "tensor")),
            P(("dp", "tensor")),
            P(("dp", "tensor")),
            P(("dp", "tensor")),
            P(("dp", "tensor")),
        ),
        check_vma=False,
    )
```

```python
import functools

import jax
import jax.numpy as jnp
from jax import lax
from jax.experimental import pallas as pl
from jax.experimental.pallas import tpu as pltpu
from jax.sharding import PartitionSpec as P

HEAD_DIM = 64
LENGTH = 1024
QUARTERS = 4
BLOCK = 256
HALF = 128
bf16 = jnp.bfloat16
f32 = jnp.float32
VMEM = pl.BlockSpec(memory_space=pltpu.VMEM)
SMEM = pl.BlockSpec(memory_space=pltpu.SMEM)
HBM = pl.BlockSpec(memory_space=pl.ANY)


RATE = 2e9
SPAN = {
    "prepare": 0.7,
    "assemble": 2.5,
    "ahead": 0.5,
    "join": 0.8,
    "pack_in": 2.5,
    "attend": 10.0,
    "pack_out": 1.6,
    "vectors": 1.6,
    "project": 5.0,
    "forward": 8.0,
    "second": 4.0,
    "backward": 10.5,
    "weights": 5.6,
    "first": 4.6,
    "output_grad": 2.9,
    "attend_back": 6.5,
    "token_grad": 0.1,
    "input_grad": 0.9,
}

ROOM = {"attend": 28, "project": 14, "forward": 26, "backward": 30, "weights": 16, "attend_back": 24}


def shape(dims, dtype):
    return jax.ShapeDtypeStruct(dims, dtype)


def call(kernel, name, operands, specs, outs, scratch=(), grid=()):
    return pl.pallas_call(
        kernel,
        grid=grid,
        name=name,
        out_shape=outs,
        in_specs=specs,
        out_specs=[VMEM] * len(outs),
        scratch_shapes=list(scratch),
        compiler_params=pltpu.CompilerParams(vmem_limit_bytes=ROOM.get(name, 12) << 20),
        cost_estimate=pl.CostEstimate(
            flops=int(SPAN[name] * RATE), bytes_accessed=0, transcendentals=0
        ),
    )(*operands)


def dot(left, right, dims=((1,), (0,))):
    return lax.dot_general(left, right, (dims, ((), ())), preferred_element_type=f32)


NT = ((1,), (1,))
TN = ((0,), (0,))


def norm_back(grad, normed, scale, gain):
    scaled = grad * gain
    return scale * (
        scaled
        - jnp.mean(scaled, -1, keepdims=True)
        - normed * jnp.mean(scaled * normed, -1, keepdims=True)
    )


def lanes(ids, j):
    return pl.ds(pl.multiple_of((ids[0] ^ j) * BLOCK, BLOCK), BLOCK)


def segments(ids, docs, dims, axis):
    place = lax.broadcasted_iota(jnp.int32, dims, axis)
    place = ((ids[2] - (place >> 8) + QUARTERS) & (QUARTERS - 1)) * BLOCK + (place & (BLOCK - 1))
    bound = docs[0, 0]
    total = (place >= bound).astype(jnp.int32)
    for j in range(1, 8):
        bound = bound + docs[0, j]
        total = total + (place >= bound).astype(jnp.int32)
    return total


SPLIT = (896, 512, 512, 512)
PLACES = (
    (("first", 0), ("x0", 0), ("y0", 0), ("y1", 1184), ("x1", 1184)),
    (("z1", 0), ("x1", 0), ("y1", 0), ("y2", 1184), ("x2", 1184)),
    (("z2", 0), ("x2", 0), ("y2", 0), ("y3", 1184), ("x3", 1184)),
    (("z3", 0), ("x3", 0), ("y3", 0), ("y4", 0), ("x4", 0)),
)
AHEAD = (("ahead", 0), ("x1", 1856), ("y1", 2080), ("y2", 1696))
EARLY = ("first", "x0", "y0", "z1", "x1", "y1", "x2", "y2", "ahead")
MIDDLE = EARLY + ("z2", "x3", "y3")
WEIGHTS = MIDDLE[:8] + MIDDLE[9:]
LAST = ("z3", "x3", "y3", "x4", "y4")
ALL = WEIGHTS + ("z3", "x4", "y4")


def find(blocks, k, j, row):
    part = j
    if j == 3 and row >= SPLIT[k]:
        part, row = 4, row - SPLIT[k]
    name, start = PLACES[k][part]
    return blocks[name], start + row


def find_ahead(blocks, k, j, row):
    if k < 3:
        return find(blocks, k, j, SPLIT[k] + 512 + row)
    name, start = AHEAD[j]
    return blocks[name], start + row


def prepare_kernel(ids, six, two, inner, wo, out):
    out[:BLOCK, :] = wo[...]
    out[BLOCK:, :] = jnp.zeros((32, HALF), bf16)
    size = six.shape[1]
    row = lax.broadcasted_iota(jnp.int32, (size, HALF), 0)
    col = lax.broadcasted_iota(jnp.int32, (size, HALF), 1)
    here = (col == row + ids[2] * size).astype(bf16)
    out[BLOCK : BLOCK + 6, :] = dot(six[...], here).astype(bf16)
    for half in range(2):
        here = (col + half * HALF == row + ids[3] * size).astype(bf16)
        at = BLOCK + half * 16
        out[at + 6 : at + 8, :] = dot(two[...], here).astype(bf16)
    out[BLOCK + 8 : BLOCK + 9, :] = inner[...]


def assemble_kernel(ids, w1, r1, w2, r2, p, rp, wq, wk, wv, tokens, first, block, sems):
    core = ids[1]
    copies = []

    def put(source, out, rows, size, cols=None):
        to = out.at[pl.ds(rows, size)] if cols is None else out.at[pl.ds(rows, size), cols]
        copies.append(pltpu.make_async_copy(source, to, sems.at[len(copies)]))

    for side, v1, v2, v in ((core, w1, w2, p), (1 - core, r1, r2, rp)):
        cols = pl.ds(pl.multiple_of(side * HALF, HALF), HALF)
        wide = pl.ds(pl.multiple_of(core * 512, 512), 512)
        for out, w2_at in ((first, 896), (block, 512)):
            for half in range(2):
                from_cols = pl.ds(pl.multiple_of(core * 512 + half * BLOCK, BLOCK), BLOCK)
                at = pl.multiple_of(half * BLOCK + side * HALF, HALF)
                put(v1.at[:, from_cols], out, at, HALF)
            put(v2.at[wide], out, w2_at, 512, cols)
            put_rest(put, core, side, v, out, w2_at + 512)
    for i, piece in enumerate((wq, wk, wv)):
        put(piece, first, 512 + i * HALF, HALF)
    for j in range(4):
        put(tokens.at[:, pl.ds(j * BLOCK, BLOCK)], block, 1184 + j * BLOCK, BLOCK)
    for copy in copies:
        copy.start()
    for copy in copies:
        copy.wait()


def join_kernel(spans, *refs):
    outs = refs[len(refs) - len(spans) :]
    for out, pieces in zip(outs, spans):
        at = 0
        for n, row, size in pieces:
            out[at : at + size, :] = refs[n][row : row + size, :]
            at += size


def put_rest(put, core, side, v, out, row):
    deep = pl.ds(pl.multiple_of(core * HALF, HALF), HALF)
    put(v.at[deep], out, row, HALF, pl.ds(pl.multiple_of(side * HALF, HALF), HALF))
    for half in range(2):
        piece = v.at[pl.ds(BLOCK + half * 16, 16)]
        at = pl.multiple_of(row + HALF + side * 16, 16)
        put(piece, out, at, 16, pl.ds(half * HALF, HALF))


def ahead_kernel(ids, p, rp, out, sems):
    core = ids[1]
    copies = []

    def put(source, out, rows, size, cols):
        to = out.at[pl.ds(rows, size), cols]
        copies.append(pltpu.make_async_copy(source, to, sems.at[len(copies)]))

    put_rest(put, core, core, p, out, 0)
    put_rest(put, core, 1 - core, rp, out, 0)
    for copy in copies:
        copy.start()
    for copy in copies:
        copy.wait()


def pack_in_kernel(p0, p1, p2, far_x, far_y, out, bias):
    total = jnp.zeros((2, BLOCK), f32)
    for j in range(4):
        refs = {"first": p0, "x0": p1, "y0": p2, "x1": far_x, "y1": far_y}
        part, row = find(refs, 0, j, 512)
        out[j * 384 : (j + 1) * 384, :] = part[row : row + 384, :]
        part, row = find(refs, 0, j, 1536)
        for side in range(2):
            vectors = part[row + side * 16 : row + side * 16 + 16, :].astype(f32)
            total = total + vectors[6:8, :]
    bias[...] = total


def pack_out_kernel(turns, names, *refs):
    blocks, (out, sems) = dict(zip(names, refs)), refs[len(names) :]
    copies = []
    for n, k in enumerate(turns):
        for j in range(4):
            ref, row_in = find_ahead(blocks, k, j, 0)
            i = n * 4 + j
            copies.append(
                pltpu.make_async_copy(
                    ref.at[pl.ds(row_in, HALF)], out.at[pl.ds(i * HALF, HALF)], sems.at[i]
                )
            )
    for copy in copies:
        copy.start()
    for copy in copies:
        copy.wait()


def vectors_kernel(ids, *refs):
    blocks = dict(zip(MIDDLE, refs))
    six, inner, held, sems = refs[len(MIDDLE) :]
    copies = []
    for k in range(4):
        for j in range(4):
            ref, row_in = find_ahead(blocks, k, j, HALF)
            i = k * 4 + j
            copies.append(
                pltpu.make_async_copy(
                    ref.at[pl.ds(row_in, 32)], held.at[pl.ds(i * 32, 32)], sems.at[i]
                )
            )
    for copy in copies:
        copy.start()
    inner[...] = jnp.zeros(inner.shape, f32)
    for copy in copies:
        copy.wait()
    for j in range(4):
        chip = ids[0] ^ j
        for side in range(2):
            total = jnp.zeros((8, HALF), f32)
            for k in range(4):
                row = (k * 4 + j) * 32 + side * 16
                piece = held[row : row + 16, :HALF].astype(f32)
                total = total + piece[:8, :]
                at = ((ids[2] - k + QUARTERS) & (QUARTERS - 1)) * 2 + (chip >> 1)
                lane = pl.ds(pl.multiple_of((chip & 1) * BLOCK + side * HALF, HALF), HALF)
                here = lax.broadcasted_iota(jnp.int32, (8, HALF), 0) == at
                inner[:, lane] += jnp.where(here, piece[8:9, :], 0.0)
            lane = pl.multiple_of(chip * BLOCK + side * HALF, HALF)
            six[:, pl.ds(lane, HALF)] = total


def one_hot(ids, docs):
    down = segments(ids, docs, (LENGTH, 1), 0)
    lane = lax.broadcasted_iota(jnp.int32, (LENGTH, HEAD_DIM), 1)
    same = (lane == down).astype(bf16)
    other = jnp.where((lane < 8) & (lane != down), -1e30, 0.0).astype(bf16)
    return same, other


def attend_kernel(
    ids, docs, t0, t1, t2, t3, own, other, bias, q, k, v, w, m0, m1, m2, m3, lse, qs, ks, vs, mixed
):
    core = ids[1]
    for j in range(4):
        base = (ids[0] ^ j) * BLOCK
        for source, side in ((own, core), (other, 1 - core)):
            rows = pl.ds(pl.multiple_of(base + side * HALF, HALF), HALF)
            for i in range(3):
                at = (j * 3 + i) * HALF
                w[rows, i * BLOCK : (i + 1) * BLOCK] = source[at : at + HALF, :]
    for b, t in enumerate((t0, t1, t2, t3)):
        rows = slice(b * BLOCK, (b + 1) * BLOCK)
        made = None
        for j in range(4):
            at = t.shape[0] - LENGTH + j * BLOCK
            part = dot(t[at : at + BLOCK, :], w[j * BLOCK : (j + 1) * BLOCK, :])
            made = part if made is None else made + part
        q[rows, :] = (made[:, :BLOCK] + bias[0:1, :]).astype(bf16)
        k[rows, :] = made[:, BLOCK : 2 * BLOCK].astype(bf16)
        v[rows, :] = (made[:, 2 * BLOCK :] + bias[1:2, :]).astype(bf16)
    same, apart = one_hot(ids, docs)
    for h in range(4):
        cols = slice(h * HEAD_DIM, (h + 1) * HEAD_DIM)
        qs[h, :, :HEAD_DIM] = q[:, cols] * bf16(0.125)
        qs[h, :, HEAD_DIM:] = same
        ks[h, :, :HEAD_DIM] = k[:, cols]
        ks[h, :, HEAD_DIM:] = apart
        vs[h, :, :HEAD_DIM] = v[:, cols]
        vs[h, :, HEAD_DIM:] = jnp.zeros((LENGTH, HEAD_DIM), bf16)

    def one_block(b, carry):
        rows = pl.ds(pl.multiple_of(b * BLOCK, BLOCK), BLOCK)

        def scores_of(h):
            return dot(qs[h, rows, :], ks[h], NT)

        scores = scores_of(0)
        for h in range(4):
            later = scores_of(h + 1) if h < 3 else None
            cols = slice(h * HEAD_DIM, (h + 1) * HEAD_DIM)
            top = jnp.max(scores, -1, keepdims=True)
            expo = jnp.exp(scores - top)
            total = jnp.sum(expo, -1, keepdims=True)
            made = dot(expo.astype(bf16), vs[h])[:, :HEAD_DIM] * (1.0 / total)
            mixed[rows, cols] = made.astype(bf16)
            lse[rows, h : h + 1] = top + jnp.log(total)
            scores = later
        return carry

    lax.fori_loop(0, 4, one_block, 0)
    for b, m in enumerate((m0, m1, m2, m3)):
        m[...] = mixed[b * BLOCK : (b + 1) * BLOCK, :]


def project_kernel(ids, tokens, x0, x1, x2, x3, other_a, other_b, vectors, *refs):
    blocks = dict(zip(MIDDLE, refs))
    wo, normed, scale, low, sems = refs[len(MIDDLE) :]
    core = ids[1]
    copies = []
    for n, k in enumerate((0, 3, 1, 2)):
        for j in range(4):
            ref, row_in = find_ahead(blocks, k, j, 0)
            got, at = (other_a, n * 4 + j) if n < 3 else (other_b, j)
            for i, (source, start, side) in enumerate(
                ((ref, row_in, core), (got, at * HALF, 1 - core))
            ):
                rows = pl.ds(pl.multiple_of(k * BLOCK + side * HALF, HALF), HALF)
                copies.append(
                    pltpu.make_async_copy(
                        source.at[pl.ds(start, HALF)],
                        wo.at[rows, lanes(ids, j)],
                        sems.at[(n * 4 + j) * 2 + i],
                    )
                )
    for copy in copies:
        copy.start()
    total = tokens[...].astype(f32) + vectors[0:1, :]
    for copy in copies:
        copy.wait()
    for k, x in enumerate((x0, x1, x2, x3)):
        total = total + dot(x[...], wo[k * BLOCK : (k + 1) * BLOCK, :])
    centered = total - jnp.mean(total, -1, keepdims=True)
    r = lax.rsqrt(jnp.mean(centered * centered, -1, keepdims=True) + 1e-05)
    n = centered * r
    normed[...] = n
    scale[...] = jnp.broadcast_to(r, scale.shape)
    low[...] = (n * vectors[2:3, :] + vectors[3:4, :]).astype(bf16)


def w1_of(blocks, k, j, half):
    ref, row = find(blocks, k, j, half * BLOCK)
    return ref[row : row + BLOCK, :]


def w2_of(blocks, k, j):
    ref, row = find(blocks, k, j, SPLIT[k])
    return ref[row : row + 512, :]


def part_of(rows, j):
    return rows[:, j * BLOCK : (j + 1) * BLOCK]


def arrange(ids, rows, mine, theirs):
    for j in range(4):
        rows[:BLOCK, j * BLOCK : (j + 1) * BLOCK] = mine[:, lanes(ids, j)]
        rows[BLOCK:, j * BLOCK : (j + 1) * BLOCK] = theirs[:, lanes(ids, j)]


def gelu_parts(inner):
    density = jnp.exp2(inner * inner * -0.7213475204444817) * 0.3989422804014327
    base = 1.0 + 0.2316419 * jnp.abs(inner)
    t = pl.reciprocal(base, approx=True)
    t = t * (2.0 - base * t)
    tail = 1.330274429 * t - 1.821255978
    tail = tail * t + 1.781477937
    tail = tail * t - 0.356563782
    tail = (tail * t + 0.319381530) * t * density
    phi = jnp.where(inner >= 0.0, 1.0 - tail, tail)
    return inner * phi, phi + inner * density


def forward_kernel(turns, ids, mine, theirs, bias, *refs):
    names = WEIGHTS if turns[0] == 0 else LAST
    blocks, refs = dict(zip(names, refs)), refs[len(names) :]
    if turns[0] == 0:
        start = None
    else:
        start, refs = refs[:2], refs[2:]
    active, slope, out_mine, out_theirs, rows, total = refs
    arrange(ids, rows, mine, theirs)
    if start is not None:
        arrange(ids, total, *start)

    def inner_of(n, half):
        k = turns[n]
        at = ((ids[2] - k + QUARTERS) & (QUARTERS - 1)) * 2 + ids[1]
        offset = bias[pl.ds(at, 1), half * BLOCK : (half + 1) * BLOCK]
        total = dot(part_of(rows, 0), w1_of(blocks, k, 0, half)) + offset
        for j in range(1, 4):
            total = total + dot(part_of(rows, j), w1_of(blocks, k, j, half))
        return total

    steps = [(n, half) for n in range(len(turns)) for half in range(2)]
    inner = inner_of(*steps[0])
    for i, (n, half) in enumerate(steps):
        later = inner_of(*steps[i + 1]) if i + 1 < len(steps) else None
        span = slice(half * BLOCK, (half + 1) * BLOCK)
        deep = slice(n * 512, (n + 1) * 512)
        made, grown = gelu_parts(inner)
        active[deep, span] = made.astype(bf16)
        slope[deep, span] = grown.astype(bf16)
        if half == 1:
            for j in range(4):
                part = dot(active[deep, :], w2_of(blocks, turns[n], j))
                if n == 0 and start is None:
                    total[:, j * BLOCK : (j + 1) * BLOCK] = part
                else:
                    total[:, j * BLOCK : (j + 1) * BLOCK] += part
        inner = later
    for j in range(4):
        span = slice(j * BLOCK, (j + 1) * BLOCK)
        out_mine[:, lanes(ids, j)] = total[:BLOCK, span]
        out_theirs[:, lanes(ids, j)] = total[BLOCK:, span]


def second_kernel(normed, mine, got, vectors, cot, out, grad, low, sums):
    gain, shift = vectors[4:5, :], vectors[5:6, :]
    total = normed[...] * vectors[2:3, :] + vectors[3:4, :] + (mine[...] + got[...])
    total = total + vectors[1:2, :]
    centered = total - jnp.mean(total, -1, keepdims=True)
    r = lax.rsqrt(jnp.mean(centered * centered, -1, keepdims=True) + 1e-05)
    n = centered * r
    out[...] = (n * gain + shift).astype(bf16)
    up = cot[...].astype(f32)
    back = norm_back(up, n, r, gain)
    grad[...] = back
    low[...] = back.astype(bf16)
    sums[0:1, :] = jnp.sum(back, 0, keepdims=True)
    sums[1:2, :] = jnp.sum(up * n, 0, keepdims=True)
    sums[2:3, :] = jnp.sum(up, 0, keepdims=True)


def backward_kernel(ids, mine, theirs, slope0, slope1, *refs):
    blocks = dict(zip(ALL, refs))
    back, out_mine, out_theirs, sums, rows = refs[len(ALL) :]
    arrange(ids, rows, mine, theirs)
    sums[...] = jnp.zeros(sums.shape, f32)
    for k in range(4):
        span = slice(k * 512, (k + 1) * 512)
        made = dot(part_of(rows, 0), w2_of(blocks, k, 0), NT)
        for j in range(1, 4):
            made = made + dot(part_of(rows, j), w2_of(blocks, k, j), NT)
        grown = slope0[span, :] if k < 3 else slope1[...]
        made = (made * grown.astype(f32)).astype(bf16)
        back[span, :] = made
        at = ((ids[2] - k + QUARTERS) & (QUARTERS - 1)) * 2 + ids[1]
        sums[pl.ds(at, 1), :] = jnp.sum(made.astype(f32), 0, keepdims=True)
    for j in range(4):
        for n, out in enumerate((out_mine, out_theirs)):
            total = None
            for k in range(4):
                rows_at = k * 512 + n * BLOCK
                for half in range(2):
                    cols = slice(half * BLOCK, (half + 1) * BLOCK)
                    part = dot(back[rows_at : rows_at + BLOCK, cols], w1_of(blocks, k, j, half), NT)
                    total = part if total is None else total + part
            out[:, lanes(ids, j)] = total.astype(out.dtype)


def weights_kernel(ids, active1, back1, active2, back2, mine, theirs, gmine, gtheirs, *outs):
    for j in range(4):
        at = lanes(ids, j)
        for active, back, out in ((active1, back1, outs[j]), (active2, back2, outs[4 + j])):
            left = dot(mine[:, at], back[:BLOCK, :], TN) + dot(theirs[:, at], back[BLOCK:, :], TN)
            out[:BLOCK, :] = left[:, :BLOCK].astype(bf16)
            out[BLOCK:512, :] = left[:, BLOCK:].astype(bf16)
            out[512:1024, :] = (
                dot(active[:BLOCK, :], gmine[:, at], TN)
                + dot(active[BLOCK:, :], gtheirs[:, at], TN)
            ).astype(bf16)


def first_kernel(second, mine, got, normed, scale, vectors, wo, grad, low, g0, g1, g2, g3, sums):
    hidden = second[...] + mine[...] + got[...].astype(f32)
    n = normed[...]
    back = norm_back(hidden, n, scale[:, :1], vectors[2:3, :])
    grad[...] = back
    rounded = back.astype(bf16)
    low[...] = rounded
    for k, g in enumerate((g0, g1, g2, g3)):
        g[...] = dot(rounded, wo[k * BLOCK : (k + 1) * BLOCK, :], NT).astype(bf16)
    sums[0:1, :] = jnp.sum(back, 0, keepdims=True)
    sums[1:2, :] = jnp.sum(hidden * n, 0, keepdims=True)
    sums[2:3, :] = jnp.sum(hidden, 0, keepdims=True)


def output_grad_kernel(ids, x0, x1, x2, x3, low, first, second, inner, own, send, made):
    core = ids[1]
    sums = jnp.concatenate([first[...], second[...], jnp.zeros((2, first.shape[1]), f32)], 0)
    for k, x in enumerate((x0, x1, x2, x3)):
        made[...] = dot(x[...], low[...], TN)
        for out, side in ((own, core), (send, 1 - core)):
            rows = pl.ds(pl.multiple_of(side * HALF, HALF), HALF)
            for j in range(4):
                at = j * 576 + k * 144
                out[at : at + HALF, :] = made[rows, lanes(ids, j)].astype(bf16)
    made[0:8, :] = sums
    for j in range(4):
        chip = ids[0] ^ j
        there = ((chip >> 1) == core).astype(f32)
        for k in range(4):
            at = ((ids[2] - k + QUARTERS) & (QUARTERS - 1)) * 2 + core
            row = inner[pl.ds(at, 1), :]
            row = jnp.where((chip & 1) == 0, row[:, :BLOCK], row[:, BLOCK:]) * there
            six = made[0:8, lanes(ids, j)]
            here = lax.broadcasted_iota(jnp.int32, (8, BLOCK), 0) == 6
            piece = jnp.concatenate([jnp.where(here, row, six), jnp.zeros((8, BLOCK), f32)], 0)
            at = j * 576 + k * 144 + HALF
            own[at : at + 16, :] = piece.astype(bf16)
            send[at : at + 16, :] = jnp.zeros((16, BLOCK), bf16)


def attend_back_kernel(
    heads, ids, docs, q, k, v, lse, m0, m1, m2, m3, g0, g1, g2, g3, out, sums, *scratch
):
    qs, ks, vs, gs, kt, ktot, vtot, qtot, stats = scratch
    count = len(heads)
    same, apart = one_hot(ids, docs)
    nothing = jnp.zeros((LENGTH, HEAD_DIM), bf16)
    centres = []
    for i, h in enumerate(heads):
        cols = slice(h * HEAD_DIM, (h + 1) * HEAD_DIM)
        qs[i, :, :HEAD_DIM] = q[:, cols] * bf16(0.125)
        qs[i, :, HEAD_DIM:] = same
        ks[i, :, :HEAD_DIM] = k[:, cols]
        ks[i, :, HEAD_DIM:] = apart
        vs[i, :, :HEAD_DIM] = v[:, cols]
        vs[i, :, HEAD_DIM:] = nothing
        gs[i, :, HEAD_DIM:] = nothing
        parts = []
        for b, (g, mixed) in enumerate(((g0, m0), (g1, m1), (g2, m2), (g3, m3))):
            gs[i, b * BLOCK : (b + 1) * BLOCK, :HEAD_DIM] = g[:, cols]
            product = g[:, cols].astype(f32) * mixed[:, cols].astype(f32)
            parts.append(jnp.sum(product, -1, keepdims=True))
        centres.append(jnp.concatenate(parts, 0))
        kt[i] = jnp.transpose(ks[i])
    centres.append(jnp.zeros((LENGTH, HALF - count), f32))
    stats[0] = jnp.transpose(jnp.concatenate(centres, 1))
    stats[1] = jnp.transpose(lse[...])
    vtot[...] = jnp.zeros(vtot.shape, f32)
    ktot[...] = jnp.zeros(ktot.shape, f32)

    def one_block(b, carry):
        rows = pl.ds(pl.multiple_of(b * BLOCK, BLOCK), BLOCK)

        def pair(i):
            return dot(ks[i], qs[i, rows, :], NT), dot(vs[i], gs[i, rows, :], NT)

        scores, dots = pair(0)
        for i in range(count):
            later = pair(i + 1) if i + 1 < count else (None, None)
            shares = jnp.exp(scores - stats[1, heads[i] : heads[i] + 1, rows])
            back = (shares * (dots - stats[0, i : i + 1, rows])).astype(bf16)
            vtot[i] += dot(shares.astype(bf16), gs[i, rows, :])
            ktot[i] += dot(back, qs[i, rows, :])
            qtot[i, :, rows] = dot(kt[i], back)
            scores, dots = later
        return carry

    lax.fori_loop(0, 4, one_block, 0)
    size = count * HEAD_DIM
    for i in range(count):
        made = (jnp.transpose(qtot[i])[:, :HEAD_DIM] * 0.125, ktot[i], vtot[i])
        for n, value in enumerate(made):
            at = n * size + i * HEAD_DIM
            out[:, at : at + HEAD_DIM] = value[:, :HEAD_DIM].astype(bf16)
    sums[0:1, :] = jnp.sum(out[:, :size].astype(f32), 0, keepdims=True)
    sums[1:2, :] = jnp.sum(out[:, 2 * size :].astype(f32), 0, keepdims=True)


def token_grad_kernel(low, high, w, wo, d0, d1, d2, d3, dqkv):
    for part, at in ((low, 0), (high, HALF)):
        for i in range(3):
            dqkv[:, i * BLOCK + at : i * BLOCK + at + HALF] = part[:, i * HALF : (i + 1) * HALF]
    for b, out in ((1, d1), (2, d2), (3, d3), (0, d0)):
        rows = slice(b * BLOCK, (b + 1) * BLOCK)
        out[:BLOCK, :] = dot(dqkv[rows, :], w[...], NT).astype(bf16)
        for i in range(3):
            at = b * 144 + i * 48
            out[BLOCK:, i * BLOCK : (i + 1) * BLOCK] = wo[at : at + 48, :]
        out[BLOCK:, 3 * BLOCK :] = jnp.zeros((48, BLOCK), bf16)


def input_grad_kernel(ids, t0, t1, t2, t3, dqkv, sums, own, send, made):
    core = ids[1]
    vectors = jnp.concatenate([sums[...], jnp.zeros((14, BLOCK), f32)], 0).astype(bf16)
    for j in range(4):
        for out in (own, send):
            out[j * 400 + 384 : (j + 1) * 400, :] = vectors
    for j in range(4):
        total = None
        for b, t in enumerate((t0, t1, t2, t3)):
            at = pl.multiple_of(t.shape[0] - LENGTH + (ids[0] ^ j) * BLOCK, 32)
            part = dot(t[pl.ds(at, BLOCK), :], dqkv[b * BLOCK : (b + 1) * BLOCK, :], TN)
            total = part if total is None else total + part
        made[...] = total
        for out, side in ((own, core), (send, 1 - core)):
            rows = pl.ds(pl.multiple_of(side * HALF, HALF), HALF)
            for i in range(3):
                to = j * 400 + i * HALF
                out[to : to + HALF, :] = made[rows, i * BLOCK : (i + 1) * BLOCK].astype(bf16)


def body_for(dp, tensor):
    fast = dp == 8 and tensor == 4
    ring_pairs = [(i, (i + 1) % tensor) for i in range(tensor)]

    def flip(value, bit, axis="dp", size=dp):
        return lax.ppermute(value, axis, [(i, i ^ bit) for i in range(size)])

    def ring(value):
        return lax.ppermute(value, "tensor", ring_pairs)

    def swap(value):
        return flip(value, 1)

    def sum_all(value, over_tensor=True):
        bit = dp >> 1
        while bit:
            value = value + flip(value, bit)
            bit >>= 1
        bit = 1
        while over_tensor and bit < tensor:
            value = value + flip(value, bit, "tensor", tensor)
            bit <<= 1
        return value

    def in_order(core, own, got, axis):
        return jnp.where(
            core == 0,
            jnp.concatenate([own, got], axis),
            jnp.concatenate([got, own], axis),
        )

    def after(value, *others):
        return lax.optimization_barrier((value, *others))[0]

    def assemble(ids, tokens, prepared, wq, wk, wv, w1, w2):
        pairs = [
            ((p * tensor + i), ((p ^ 1) * tensor + (i + tensor - 1) % tensor))
            for p in range(dp)
            for i in range(tensor)
        ]
        back = [(i, (i + tensor - 1) % tensor) for i in range(tensor)]
        made = call(
            assemble_kernel,
            "assemble",
            (ids, w1, swap(w1), w2, swap(w2), prepared, swap(prepared), wq, wk, wv, tokens),
            [SMEM] + [HBM] * 10,
            [shape((1568, BLOCK), bf16), shape((2208, BLOCK), bf16)],
            scratch=[pltpu.SemaphoreType.DMA((31,))],
        )
        gated = after(prepared, made[0])
        ahead = call(
            ahead_kernel,
            "ahead",
            (ids, lax.ppermute(gated, "tensor", back), lax.ppermute(gated, ("dp", "tensor"), pairs)),
            [SMEM] + [HBM] * 2,
            [shape((HALF + 32, BLOCK), bf16)],
            scratch=[pltpu.SemaphoreType.DMA((6,))],
        )[0]
        return made, ahead

    def gather_any(core, z, wq, wk, wv, wo, w1, w2):
        def whole(value, dim):
            value = lax.all_gather(value, "dp", axis=dim, tiled=True)
            return value

        def quarters(value):
            value = lax.all_gather(value, "tensor", axis=0, tiled=False)
            return jnp.take(value, (z - jnp.arange(tensor)) % tensor, axis=0)

        a = quarters(lax.dynamic_slice_in_dim(whole(w1, 0), core * 512, 512, 1))
        b = quarters(lax.dynamic_slice_in_dim(whole(w2, 1), core * 512, 512, 0))
        c = quarters(lax.dynamic_slice_in_dim(whole(wo, 1), core * HALF, HALF, 0))
        qkv = jnp.stack([whole(wq, 0), whole(wk, 0), whole(wv, 0)])
        qkv = qkv.reshape(3, 4, 2, HALF, BLOCK).transpose(2, 1, 0, 3, 4).reshape(2, 1536, BLOCK)
        blocks, parts = {}, {}
        for k in range(4):
            for j in range(4):
                span = slice(j * BLOCK, (j + 1) * BLOCK)
                left = [a[k, span, :BLOCK], a[k, span, BLOCK:]]
                if k == 0:
                    left.append(jnp.zeros((384, BLOCK), bf16))
                right = [b[k][:, span], c[k][:, span], jnp.zeros((32, BLOCK), bf16)]
                if j < 3:
                    parts[PLACES[k][j]] = left + right
                else:
                    parts[PLACES[k][3]], parts[PLACES[k][4]] = left, right
        for j in range(4):
            piece = c[3][:, j * BLOCK : (j + 1) * BLOCK]
            parts[AHEAD[j]] = [piece, jnp.zeros((32, BLOCK), bf16)]
        for name in ALL + ("ahead",):
            made = [parts[place] for place in sorted(p for p in parts if p[0] == name)]
            blocks[name] = jnp.concatenate(sum(made, []), 0)
        return blocks, qkv[core], qkv[1 - core]

    def body(
        tokens,
        cotangent,
        doc_lengths,
        query_weight,
        key_weight,
        value_weight,
        output_weight,
        inner_weight,
        outer_weight,
        query_offset,
        value_offset,
        inner_offset,
        output_offset,
        outer_offset,
        first_gain,
        first_shift,
        second_gain,
        second_shift,
    ):
        place = lax.axis_index("dp")
        z = lax.axis_index("tensor")
        core = place & 1
        chip = (place >> 1) if fast else jnp.zeros_like(place)
        ids = jnp.stack([chip, core, z, place]).astype(jnp.int32)
        rows = tokens.shape[0]
        width = tokens.shape[1]

        six = jnp.stack(
            [output_offset, outer_offset, first_gain, first_shift, second_gain, second_shift]
        )
        two = jnp.stack([query_offset, value_offset])
        weights = (query_weight, key_weight, value_weight)
        t = [tokens]
        if fast:
            prepared = call(
                prepare_kernel,
                "prepare",
                (ids, six, two, inner_offset[None], output_weight),
                [SMEM] + [VMEM] * 4,
                [shape((BLOCK + 32, HALF), bf16)],
            )[0]
            (first, block), ahead = assemble(
                ids, tokens, prepared, *weights, inner_weight, outer_weight
            )

            def join(*outs):
                inputs = []
                for _, source, _, _ in sum(outs, []):
                    if not any(source is other for other in inputs):
                        inputs.append(source)

                def index(source):
                    return [other is source for other in inputs].index(True)

                spans = [[(index(a), row, size) for _, a, row, size in out] for out in outs]
                return call(
                    functools.partial(join_kernel, spans),
                    "join",
                    tuple(inputs),
                    [VMEM] * len(inputs),
                    [shape((sum(size for _, _, size in span), BLOCK), bf16) for span in spans],
                )

            x0, y0, z1 = flip(first, 2), flip(first, 4), ring(block)
            xm, ym = join(
                [(0, z1, 0, 1184), (0, y0, 896, 672), (0, ahead, 0, 160)],
                [(0, z1, 0, 1184), (0, x0, 0, 896), (0, ahead, 0, 160)],
            )
            x1, y1, z2 = flip(xm, 2), flip(ym, 4), ring(after(z1, xm))
            xm, ym, tokens2, part2 = join(
                [(0, z2, 0, 1184), (0, y1, 512, 672)],
                [(0, z2, 0, 1184), (0, x1, 0, 512), (0, x1, 1856, 160)],
                [(0, z2, 1184, 1024)],
                [(0, z2, 0, 1184)],
            )
            x2, y2, t3, z3 = flip(xm, 2), flip(ym, 4), ring(tokens2), ring(part2)
            t = [block, z1, z2, t3]
            own_in, qv_bias = call(
                pack_in_kernel,
                "pack_in",
                (first, x0, y0, x1, y1),
                [VMEM] * 5,
                [shape((1536, BLOCK), bf16), shape((2, BLOCK), f32)],
            )
            other_in = swap(own_in)
        else:
            piece = six.shape[1]
            field = jnp.arange(width) // piece == place * tensor + z
            six = jnp.where(field, jnp.tile(six.astype(f32), (1, width // piece)), 0)
            piece = two.shape[1]
            field = jnp.arange(width) // piece == z * dp + place
            two = jnp.where(field, jnp.tile(two.astype(f32), (1, width // piece)), 0)
            piece = inner_offset.shape[0]
            wide = piece * dp * tensor
            field = jnp.arange(wide) // piece == z * dp + place
            one = jnp.where(field, jnp.tile(inner_offset.astype(f32), wide // piece), 0)
            vectors = sum_all(jnp.concatenate([six, two, one.reshape(4, width)], 0))
            qv_bias = lax.dynamic_slice(vectors, (6, z * BLOCK), (2, BLOCK))
            inner_bias = vectors[8:12].reshape(8, 512)
            vectors = vectors[:8]
            blocks, own_in, other_in = gather_any(
                core, z, *weights, output_weight, inner_weight, outer_weight
            )
            for _ in range(3):
                t.append(ring(t[-1]))
            t = [
                jnp.concatenate([p[:, j * BLOCK : (j + 1) * BLOCK] for j in range(4)], 0)
                for p in t
            ]

        square = shape((LENGTH, BLOCK), bf16)
        tile = shape((BLOCK, BLOCK), bf16)
        q, k, v, w_in, m0, m1, m2, m3, lse = call(
            attend_kernel,
            "attend",
            (ids, doc_lengths, *t, own_in, other_in, qv_bias),
            [SMEM, SMEM] + [VMEM] * 7,
            [square] * 3
            + [shape((width, 3 * BLOCK), bf16)]
            + [tile] * 4
            + [shape((LENGTH, HALF), f32)],
            scratch=[pltpu.VMEM((4, LENGTH, HALF), bf16)] * 3 + [pltpu.VMEM((LENGTH, BLOCK), bf16)],
        )

        def shift(value, by):
            return lax.ppermute(value, "tensor", [(i, (i - by) % tensor) for i in range(tensor)])

        if fast:
            z3, x2, y2, m0 = lax.optimization_barrier((z3, x2, y2, m0))
            xm, ym = join(
                [(0, z3, 0, 1184), (0, y2, 512, 672)],
                [(0, z3, 0, 1184), (0, x2, 0, 512)],
            )
            x3, y3 = flip(xm, 2), flip(ym, 4)
        x = [m0, shift(m3, 3), shift(m2, 2), shift(m1, 1)]

        def pack_out(turns, names):
            size = len(turns) * 4
            return swap(
                call(
                    functools.partial(pack_out_kernel, turns, names),
                    "pack_out",
                    tuple(blocks[name] for name in names),
                    [HBM] * len(names),
                    [shape((size * HALF, BLOCK), bf16)],
                    scratch=[pltpu.SemaphoreType.DMA((size,))],
                )[0]
            )

        if fast:
            blocks = {
                "first": first,
                "x0": x0,
                "y0": y0,
                "z1": z1,
                "x1": x1,
                "y1": y1,
                "z2": z2,
                "x2": x2,
                "y2": y2,
                "ahead": ahead,
            }
        other_a = pack_out((0, 3, 1), EARLY)
        if fast:
            x3, y3, *x = lax.optimization_barrier((x3, y3, *x))
            xm, ym = join([(0, y3, 512, 672)], [(0, x3, 0, 512)])
            blocks.update(z3=z3, x3=x3, y3=y3, x4=flip(xm, 2), y4=flip(ym, 4))
            vectors, inner_bias = call(
                vectors_kernel,
                "vectors",
                (ids, *[blocks[name] for name in MIDDLE]),
                [SMEM] + [HBM] * len(MIDDLE),
                [shape((8, width), f32), shape((8, 512), f32)],
                scratch=[pltpu.VMEM((512, BLOCK), bf16), pltpu.SemaphoreType.DMA((16,))],
            )
        other_b = pack_out((2,), MIDDLE)
        wide_f = shape((rows, width), f32)
        wide_b = shape((rows, width), bf16)
        w_out, normed1, scale1, hidden_low = call(
            project_kernel,
            "project",
            (ids, tokens, *x, other_a, other_b, vectors, *[blocks[name] for name in MIDDLE]),
            [SMEM] + [VMEM] * 5 + [HBM] * 2 + [VMEM] + [HBM] * len(MIDDLE),
            [shape((width, width), bf16), wide_f, shape((rows, HALF), f32), wide_b],
            scratch=[pltpu.SemaphoreType.DMA((32,))],
        )
        hidden_other = swap(hidden_low)

        def forward(turns, *start):
            tall = shape((len(turns) * 512, 512), bf16)
            names = WEIGHTS if turns[0] == 0 else LAST
            return call(
                functools.partial(forward_kernel, turns),
                "forward",
                (ids, hidden_low, hidden_other, inner_bias)
                + tuple(blocks[name] for name in names)
                + start,
                [SMEM] + [VMEM] * (3 + len(names) + len(start)),
                [tall, tall, wide_f, wide_f],
                scratch=[
                    pltpu.VMEM((2 * rows, width), bf16),
                    pltpu.VMEM((2 * rows, width), f32),
                ],
            )

        active0, slope0, out_own, out_send = forward((0, 1, 2))
        active1, slope1, out_own, out_send = forward((3,), out_own, out_send)
        result, second_grad, second_low, second_sums = call(
            second_kernel,
            "second",
            (
                normed1,
                out_own,
                swap(out_send),
                vectors,
                cotangent,
            ),
            [VMEM] * 5,
            [wide_b, wide_f, wide_b, shape((3, width), f32)],
        )
        second_other = swap(second_low)
        tall = shape((2048, 512), bf16)
        back, grad_own, grad_send, inner_sums = call(
            backward_kernel,
            "backward",
            (ids, second_low, second_other, slope0, slope1, *[blocks[name] for name in ALL]),
            [SMEM] + [VMEM] * (4 + len(ALL)),
            [tall, wide_f, wide_b, shape((8, 512), f32)],
            scratch=[pltpu.VMEM((2 * rows, width), bf16)],
        )

        def weights_of(turns, *others):
            def at(turn):
                return pl.BlockSpec((512, 512), lambda i: (turn, 0))

            def active_of(turn):
                return (active0, at(turn)) if turn < 3 else (active1, at(0))

            (a, a_at), (b, b_at) = active_of(turns[0]), active_of(turns[1])
            made = call(
                weights_kernel,
                "weights",
                (
                    ids,
                    a,
                    back,
                    b,
                    back,
                    hidden_low,
                    hidden_other,
                    second_low,
                    after(second_other, *others),
                ),
                [SMEM, a_at, at(turns[0]), b_at, at(turns[1])] + [VMEM] * 4,
                [shape((1024, BLOCK), bf16)] * 8,
                grid=(1,),
            )
            return {turns[0]: made[:4], turns[1]: made[4:]}

        grad_got = swap(grad_send)
        grads = weights_of((1, 2))
        first_grad, first_low, g0, g1, g2, g3, first_sums = call(
            first_kernel,
            "first",
            (
                second_grad,
                grad_own,
                after(grad_got, *grads[1]),
                normed1,
                scale1,
                vectors,
                w_out,
            ),
            [VMEM] * 7,
            [wide_f, wide_b] + [tile] * 4 + [shape((3, width), f32)],
        )
        g = [g0, shift(g3, 3), shift(g2, 2), shift(g1, 1)]
        grads.update(weights_of((3, 0), first_low))

        def meet(parts, turn):
            own, by_x, by_y, far = parts
            if turn % 2 == 0:
                return [own, by_x + flip(far, 4), by_y]
            return [own, by_x, by_y + flip(far, 2)]

        out_part = shape((2304, BLOCK), bf16)
        wo_own, wo_send = call(
            output_grad_kernel,
            "output_grad",
            (ids, *x, first_low, first_sums, second_sums, inner_sums),
            [SMEM] + [VMEM] * 8,
            [out_part, out_part],
            scratch=[pltpu.VMEM((BLOCK, width), f32)],
        )
        if fast:
            gated = lax.optimization_barrier(
                (grads[1][2], grads[2][1], grads[3][3], grads[0][3], *g[1:])
            )
            grads[1], grads[2] = list(grads[1]), list(grads[2])
            grads[3], grads[0] = list(grads[3]), list(grads[0])
            grads[1][2], grads[2][1] = gated[:2]
            met = {turn: meet(grads[turn], turn) for turn in (1, 2)}
            wo_got = swap(wo_send)

            def send(turn):
                return flip(met[turn][1], 2), flip(met[turn][2], 4)

            sent = {1: send(1)}

            def settle(turn, moving=None):
                total = (
                    met[turn][0].astype(f32)
                    + sent[turn][0].astype(f32)
                    + sent[turn][1].astype(f32)
                )
                return total if moving is None else total + moving.astype(f32)

        def attend_back(heads, g):
            size = len(heads) * HEAD_DIM
            return call(
                functools.partial(attend_back_kernel, heads),
                "attend_back",
                (ids, doc_lengths, q, k, v, lse, m0, m1, m2, m3, *g),
                [SMEM, SMEM] + [VMEM] * 12,
                [shape((LENGTH, 3 * size), bf16), shape((2, size), f32)],
                scratch=[pltpu.VMEM((len(heads), LENGTH, HALF), bf16)] * 4
                + [pltpu.VMEM((len(heads), HALF, LENGTH), bf16)]
                + [pltpu.VMEM((len(heads), LENGTH, HALF), f32)] * 2
                + [pltpu.VMEM((len(heads), HALF, LENGTH), f32)]
                + [pltpu.VMEM((2, HALF, LENGTH), f32)],
            )

        if fast:
            wo_total = (wo_own.astype(f32) + wo_got.astype(f32)).astype(bf16)
            wo_parts = [wo_total[j * 576 : (j + 1) * 576] for j in range(4)]
            wo_far = flip(wo_parts[3], 2)
            g[0] = after(g[0], met[1][2], met[2][1], wo_far)
        dqkv_low, sums_low = attend_back((0, 1), g)
        if fast:
            wo_x = flip(wo_parts[1], 2)
            wo_y = flip(wo_parts[2] + wo_far, 4)
            gated = (*sent[1], *met[2][1:3], grads[3][3], grads[0][3], dqkv_low)
            gated = lax.optimization_barrier(gated)
            sent[1] = gated[:2]
            met[2][1:3] = gated[2:4]
            grads[3][3], grads[0][3] = gated[4:6]
            sent[2] = send(2)
            total1 = settle(1).astype(bf16)
            moving1 = ring(total1)
            g[0] = after(g[0], dqkv_low, total1)
        dqkv_high, sums_high = attend_back((2, 3), g)
        head_sums = jnp.concatenate([sums_low, sums_high], 1)
        if fast:
            wo_total = wo_parts[0].astype(f32) + wo_x.astype(f32) + wo_y.astype(f32)
            wo_total = after(wo_total.astype(bf16), dqkv_high)
        else:
            wo_total = wo_own[:576]
        moved = shape((rows + 48, width), bf16)
        d0, d1, d2, d3, dqkv = call(
            token_grad_kernel,
            "token_grad",
            (dqkv_low, dqkv_high, w_in, wo_total),
            [VMEM] * 4,
            [moved] * 4 + [shape((LENGTH, 3 * BLOCK), bf16)],
        )
        if fast:
            gated = lax.optimization_barrier((*grads[3][1:3], *grads[0][1:3], d1))
            met[3] = meet([grads[3][0], *gated[0:2], grads[3][3]], 3)
            met[0] = meet([grads[0][0], *gated[2:4], grads[0][3]], 0)
            sent.update({turn: send(turn) for turn in (3, 0)})
            total2 = settle(2, moving1).astype(bf16)
            moving2 = ring(total2)
            dqkv = after(dqkv, met[3][2], met[0][1])
        in_part = shape((1600, BLOCK), bf16)
        in_own, in_send = call(
            input_grad_kernel,
            "input_grad",
            (ids, *t, dqkv, head_sums),
            [SMEM] + [VMEM] * 6,
            [in_part, in_part],
            scratch=[pltpu.VMEM((BLOCK, 3 * BLOCK), f32)],
        )

        def add(left, right):
            return (left.astype(f32) + right.astype(f32)).astype(bf16)

        moving = ring(d1)
        if fast:
            moving, in_send = lax.optimization_barrier((moving, in_send))
            moving = ring(add(moving, d2))
            total3 = settle(3, moving2).astype(bf16)
            moving3 = ring(total3)
            in_total = add(in_own, swap(in_send))
            in_parts = [in_total[j * 400 : (j + 1) * 400] for j in range(4)]
            in_far = flip(in_parts[3], 6)
            moving = ring(add(moving, d3))
            in_x = flip(in_parts[1], 2)
            in_y = flip(in_parts[2], 4)
            mine = settle(0, moving3)
        else:
            moving = ring(add(moving, d2))
            moving = ring(add(moving, d3))
        moving = moving.astype(f32) + d0.astype(f32)
        tokens_grad = first_grad + moving[:rows]

        if fast:
            left = mine[:512].reshape(2, 2, HALF, BLOCK)
            right = mine[512:]

            def sides(side):
                a = lax.dynamic_index_in_dim(left, side, 1, False)
                b = lax.dynamic_slice_in_dim(right, side * HALF, HALF, 1)
                return a, b

            a, b = sides(1 - core)
            got = swap(
                jnp.concatenate(
                    [a[0, :, :HALF], a[0, :, HALF:], a[1, :, :HALF], a[1, :, HALF:], b], 0
                ).astype(bf16)
            ).astype(f32)
            a, b = sides(core)
            ga = jnp.concatenate([got[i * HALF : (i + 1) * HALF] for i in range(4)], 1)
            inner_grad = in_order(core, jnp.concatenate([a[0], a[1]], 1), ga, 1)
            outer_grad = in_order(core, b, got[512:], 0)

            total = jnp.concatenate(
                [moving[rows:, i * BLOCK : (i + 1) * BLOCK] for i in range(3)], 0
            )
            got = swap(lax.dynamic_slice_in_dim(total, (1 - core) * HALF, HALF, 1))
            total = lax.dynamic_slice_in_dim(total, core * HALF, HALF, 1)
            output_grad = in_order(core, total[:HALF], got[:HALF], 0)
            sums = total[HALF:] + got[HALF:]
            six = lax.dynamic_slice(sums, (0, z * 32), (6, 32))
            offset_inner = sums[6]

            total = in_parts[0].astype(f32) + in_x.astype(f32)
            total = total + in_y.astype(f32) + in_far.astype(f32)
            query_grad, key_grad, value_grad = [
                total[i * HALF : (i + 1) * HALF] for i in range(3)
            ]
            head_sums = total[384:386]
        else:
            def scatter(value, dim):
                return lax.psum_scatter(value, "dp", scatter_dimension=dim, tiled=True)

            def quarter(parts):
                found = jnp.stack(parts).astype(f32)
                found = jnp.take(found, (z - jnp.arange(tensor)) % tensor, axis=0)
                return lax.psum_scatter(found, "tensor", scatter_dimension=0, tiled=False)

            def half(value, dim):
                field = jnp.zeros_like(value)
                return jnp.where(
                    core == 0,
                    jnp.concatenate([value, field], dim),
                    jnp.concatenate([field, value], dim),
                )

            a = quarter(
                [
                    jnp.concatenate(
                        [jnp.concatenate([p[:BLOCK], p[BLOCK:512]], 1) for p in grads[turn]], 0
                    )
                    for turn in range(4)
                ]
            )
            b = quarter(
                [jnp.concatenate([p[512:1024] for p in grads[turn]], 1) for turn in range(4)]
            )
            inner_grad = scatter(half(a, 1), 0)
            outer_grad = scatter(half(b, 0), 1)

            def heads(value):
                value = value.reshape(4, 4, 144, BLOCK)[:, :, :HALF]
                return value.transpose(1, 2, 0, 3).reshape(4, HALF, width)

            mine, theirs = quarter(list(heads(wo_own))), quarter(list(heads(wo_send)))
            output_grad = scatter(in_order(core, mine, theirs, 0), 1)
            own, send = [
                p.astype(f32).reshape(4, 400, BLOCK)[:, :384].reshape(4, 3, HALF, BLOCK)
                for p in (in_own, in_send)
            ]
            both = jnp.where(core == 0, jnp.stack([own, send], 1), jnp.stack([send, own], 1))
            both = both.transpose(2, 0, 1, 3, 4).reshape(3, width, BLOCK)
            query_grad, key_grad, value_grad = [scatter(both[i], 0) for i in range(3)]

            sums = jnp.concatenate([first_sums, second_sums, inner_sums.reshape(4, width)], 0)
            sums = sum_all(sums)
            head_sums = sum_all(head_sums, False)
            piece = width // (dp * tensor)
            six = lax.dynamic_slice_in_dim(sums[:6], (place * tensor + z) * piece, piece, 1)
            piece = inner_offset.shape[0]
            offset_inner = lax.dynamic_slice_in_dim(
                sums[6:].reshape(-1), (z * dp + place) * piece, piece, 0
            )

        head_sums = lax.dynamic_slice_in_dim(head_sums, place * (BLOCK // dp), BLOCK // dp, 1)
        return (
            result,
            tokens_grad,
            query_grad,
            key_grad,
            value_grad,
            output_grad,
            inner_grad,
            outer_grad,
            head_sums[0],
            head_sums[1],
            offset_inner,
            six[0],
            six[3],
            six[1],
            six[2],
            six[4],
            six[5],
        )

    return body


def solution(mesh):
    return jax.shard_map(
        body_for(mesh.shape["dp"], mesh.shape["tensor"]),
        mesh=mesh,
        in_specs=(
            P(("dp", "tensor"), None),
            P(("dp", "tensor"), None),
            P("dp", None),
            P("dp", "tensor"),
            P("dp", "tensor"),
            P("dp", "tensor"),
            P("tensor", "dp"),
            P("dp", "tensor"),
            P("tensor", "dp"),
            P(("tensor", "dp")),
            P(("tensor", "dp")),
            P(("tensor", "dp")),
            P(("dp", "tensor")),
            P(("dp", "tensor")),
            P(("dp", "tensor")),
            P(("dp", "tensor")),
            P(("dp", "tensor")),
            P(("dp", "tensor")),
        ),
        out_specs=(
            P(("dp", "tensor"), None),
            P(("dp", "tensor"), None),
            P("dp", "tensor"),
            P("dp", "tensor"),
            P("dp", "tensor"),
            P("tensor", "dp"),
            P("dp", "tensor"),
            P("tensor", "dp"),
            P(("tensor", "dp")),
            P(("tensor", "dp")),
            P(("tensor", "dp")),
            P(("dp", "tensor")),
            P(("dp", "tensor")),
            P(("dp", "tensor")),
            P(("dp", "tensor")),
            P(("dp", "tensor")),
            P(("dp", "tensor")),
        ),
        check_vma=False,
    )
```
